128 devices in a mesh: section: 16 (over x, z_hi, core), tp: 8 (over y, z_lo).
Axes of the slice: x: 4, y: 4, z: 4 (z_hi: 2, z_lo: 2; z = z_hi * 2 + z_lo), core: 2. Of those that a mesh axis runs over, the one named last changes fastest.
Arguments:
- fresh_input: bfloat16 [1024, 3072], P(None, 'tp'), may hold values from -80 to 80
- previous_out: bfloat16 [16384, 3072], P('section', 'tp'), may hold values from -80 to 80
- norm_gain: bfloat16 [16, 3072], P('section', 'tp'), may hold values from 0.099609375 to 1.8984375
- gate_weight: bfloat16 [16, 3072, 8192], P('section', None, 'tp'), may hold values from -0.109375 to 0.109375
- up_weight: bfloat16 [16, 3072, 8192], P('section', None, 'tp'), may hold values from -0.109375 to 0.109375
- down_weight: bfloat16 [16, 8192, 3072], P('section', 'tp'), may hold values from -0.25 to 0.25
Outputs:
- section_out: bfloat16 [16384, 3072], P('section', 'tp')
The draws below stay inside these ranges and needn't reach their ends.
All inputs are finite; a program needn't handle non-finite values.
Results may differ from the reference program's by a relative error of at most 0.015.
Values may be sent and summed in bfloat16 or wider, within the bound.
A program may use at most 128 MiB of HBM per device.

```python
import math
import jax
import jax.numpy as jnp
from jax import lax

D = 3072
FF = 8192
TOK = 1024
SECTIONS = 16
H_DEV = 1024
ROWS = 16384
N_TP = 8


def scaled_field(key, row_count, col_count, ramp_span, values):
    key_rows, key_cols = jax.random.split(key, 2)
    row_scale = jnp.exp(jax.random.uniform(key_rows, (row_count, 1), jnp.float32, math.log(0.3), math.log(3.0)))
    position = jnp.arange(col_count, dtype=jnp.float32) / col_count
    col_log = jax.random.uniform(key_cols, (1, col_count), jnp.float32, math.log(0.4), math.log(2.5))
    col_scale = jnp.exp(col_log + math.log(ramp_span) * (position[None, :] - 0.5))
    return values * row_scale * col_scale


def draw_fresh_input(key, part):
    key = jax.random.fold_in(key, 11)
    key_field, key_values = jax.random.split(key, 2)
    values = jnp.clip(jax.random.normal(key_values, (TOK, D), jnp.float32), -6.0, 6.0)
    field_out = scaled_field(key_field, TOK, D, 3.0, values)
    return field_out.astype(jnp.bfloat16)


def draw_previous_out(key, part):
    key = jax.random.fold_in(key, 23)
    key_field, key_values = jax.random.split(key, 2)
    values = jnp.clip(jax.random.normal(key_values, (ROWS, D), jnp.float32), -6.0, 6.0)
    field_out = scaled_field(key_field, ROWS, D, 3.0, values)
    return field_out.astype(jnp.bfloat16)


def strengthened(values, key, source, target, blocks, factor):
    owner, partner = [(jnp.arange(values.shape[dim]) // (values.shape[dim] // blocks)).reshape([-1 if axis == dim else 1 for axis in range(values.ndim)]) for dim in (source, target)]
    chosen = jax.random.permutation(key, blocks)[partner]
    strong = (owner == chosen) | (owner == (partner + blocks // 2) % blocks)
    return jnp.where(strong, factor * values, values)


def block_scale(own_key, extent, cuts, least, top_value):
    def one(axis_at, parts):
        draws = jax.random.uniform(jax.random.fold_in(jax.random.fold_in(own_key, 6), axis_at), (parts,), jnp.float32, least / len(cuts), top_value / len(cuts))
        return jnp.repeat(jnp.exp(draws), extent[axis_at] // parts).reshape((-1,) + (1,) * (len(extent) - axis_at - 1))

    level = one(*cuts[0])
    for cut in cuts[1:]:
        level = level * one(*cut)
    return level


def gaussian(rng, shape, scale, reach, pieces=(), kind=jnp.bfloat16):
    array = jax.random.normal(rng, shape, jnp.float32) * scale
    if len(pieces) > 0:
        array = block_scale(rng, shape, pieces, -0.22, 0.18) * array
    return jnp.clip(array, min=-reach, max=reach).astype(kind)


def noise_with(key, extent, scale, bound, cuts, heavy, kind=jnp.bfloat16):
    drawn = scale * jax.random.normal(key, extent, jnp.float32)
    if cuts:
        drawn = drawn * block_scale(key, extent, cuts, -0.22, 0.18)
    return jnp.clip(strengthened(drawn, jax.random.fold_in(key, 3), *heavy), -bound, bound).astype(kind)


def setup_inputs(seed: int = 0) -> dict:
    keys = jax.random.split(jax.random.key(seed), 7)
    return {
        "fresh_input": draw_fresh_input(jax.random.fold_in(keys[6], 71), 0),
        "previous_out": draw_previous_out(jax.random.fold_in(keys[6], 71), 0),
        "norm_gain": jnp.clip(1.0 + 0.18 * jax.random.normal(keys[2], (SECTIONS, D), jnp.float32), 0.099609375, 1.8984375).astype(jnp.bfloat16),
        "gate_weight": gaussian(keys[3], (SECTIONS, D, FF), D ** -0.5, 0.109375, ((0, 16), (2, 8))),
        "up_weight": gaussian(keys[4], (SECTIONS, D, FF), D ** -0.5, 0.109375, ((0, 16), (2, 8))),
        "down_weight": noise_with(keys[5], (SECTIONS, FF, D), H_DEV ** -0.5, 0.25, ((0, 16), (1, 8)), (1, 2, 8, 2.0)),
    }


EPSILON = 1e-05
BLOCK_EPSILON = 1e-06
CLIP_FACTOR = 2.0

def hadamard_table():
    indices = jnp.arange(128, dtype=jnp.int32)
    intersection = indices[:, None] & indices[None, :]
    parity = jnp.zeros_like(intersection)
    for bit_pos in range(7):
        parity = parity + (intersection >> bit_pos & 1)
    sign_table = 1 - 2 * (parity % 2)
    return sign_table.astype(jnp.float32) / math.sqrt(128.0)

def rotate(values, hadamard):
    dims_now = values.shape
    blocks = values.reshape(dims_now[:-1] + (dims_now[-1] // 128, 128))
    turned = jnp.einsum('...k,kj->...j', blocks, hadamard, precision=lax.Precision.HIGHEST)
    return turned.reshape(dims_now)

def saturate(values):
    dims_now = values.shape
    blocks = values.reshape(dims_now[:-1] + (dims_now[-1] // 128, 128))
    limit = CLIP_FACTOR * jnp.sqrt(lax.optimization_barrier(jnp.mean(blocks * blocks, axis=-1, keepdims=True)) + BLOCK_EPSILON)
    return jnp.clip(blocks, -limit, limit).reshape(dims_now)

def reference(fresh_input, previous_out, norm_gain, gate_weight, up_weight, down_weight):
    hadamard = hadamard_table()
    section_rows = previous_out.reshape(SECTIONS, TOK, D)
    incoming = jnp.concatenate([fresh_input[None], section_rows[:-1]], axis=0)

    def one_section(inputs):
        current, gain_row, w_gate, w_up, w_down = inputs
        wide_rows = current.astype(jnp.float32)
        mean_square = lax.optimization_barrier(jnp.mean(wide_rows * wide_rows, axis=1, keepdims=True))
        normed = (wide_rows * lax.rsqrt(mean_square + EPSILON) * gain_row.astype(jnp.float32)[None, :]).astype(jnp.bfloat16)
        gate_out = jnp.dot(normed, w_gate, preferred_element_type=jnp.float32)
        up_out = jnp.dot(normed, w_up, preferred_element_type=jnp.float32)
        hidden = (jax.nn.silu(gate_out) * up_out).astype(jnp.bfloat16)
        hidden_groups = jnp.transpose(hidden.reshape(TOK, N_TP, H_DEV), (1, 0, 2))
        down_groups = w_down.reshape(N_TP, H_DEV, D)

        def one_group(pair):
            group_hidden, group_down = pair
            term_full = jnp.dot(group_hidden, group_down, preferred_element_type=jnp.float32)
            return saturate(rotate(term_full, hadamard)).astype(jnp.bfloat16)
        rotated = lax.map(one_group, (hidden_groups, down_groups))
        total_sum = lax.optimization_barrier(jnp.sum(rotated.astype(jnp.float32), axis=0))
        update = rotate(total_sum, hadamard)
        return (wide_rows + update).astype(jnp.bfloat16)
    outputs = lax.map(one_section, (incoming, norm_gain, gate_weight, up_weight, down_weight))
    return outputs.reshape(SECTIONS * TOK, D)
```

```python
import math

import jax
import jax.numpy as jnp
from jax import lax
from jax.experimental import pallas as pl
from jax.experimental.pallas import tpu as pltpu
from jax.sharding import PartitionSpec as P

EPSILON = 1e-05
BLOCK_EPSILON = 1e-06
CLIP_FACTOR = 2.0

MESH = pl.DeviceIdType.MESH
F32 = jnp.float32
BF16 = jnp.bfloat16

TOK = 1024
D = 3072
H_DEV = 1024
PART = 384
ROWS = 256
CHUNKS = TOK // ROWS
TILE = 256
COPIES = 30

LO, HALF, HI = 48, 128, 192


def kernel(
    fresh_ref, prev_ref, gain_ref, gate_ref, up_ref, down_ref, out_ref,
    xg, wg, wu, wd, rot, land1, land2, land3, nb, hb, gains, hada, ones,
    load_sem, fresh_sem, relay_send, relay_recv, gain_send, gain_recv, send, recv,
):
    s = lax.axis_index("section")
    t = lax.axis_index("tp")
    n_sections = lax.axis_size("section")
    n_tp = lax.axis_size("tp")
    y, z = t // 2, t % 2
    core = s % 2
    yp, ym, yf = (y + 1) % 4, (y + 3) % 4, (y + 2) % 4
    zb = 1 - z
    dev_p, dev_m, dev_z = (s, yp * 2 + z), (s, ym * 2 + z), (s, y * 2 + zb)
    has_next = s < n_sections - 1
    has_prev = s > 0
    next_dev = (jnp.minimum(s + 1, n_sections - 1), jnp.where(core == 0, t, y * 2 + zb))
    prev_dev = (jnp.maximum(s - 1, 0), jnp.where(core == 1, t, y * 2 + zb))
    zo = jnp.where(jnp.logical_or(core == 1, s == 0), z, zb)
    zq = 1 - zo

    loads = [
        pltpu.make_async_copy(src, dst, load_sem.at[i])
        for i, (src, dst) in enumerate(((down_ref.at[0], wd), (gate_ref.at[0], wg), (up_ref.at[0], wu)))
    ]
    for load in loads:
        load.start()

    barrier = pltpu.get_barrier_semaphore()
    for q in range(1, n_tp):
        pl.semaphore_signal(barrier, inc=1, device_id=(s, (t + q) % n_tp), device_id_type=MESH)

    @pl.when(has_next)
    def _():
        pl.semaphore_signal(barrier, inc=1, device_id=next_dev, device_id_type=MESH)

    @pl.when(has_prev)
    def _():
        pl.semaphore_signal(barrier, inc=1, device_id=prev_dev, device_id_type=MESH)

    pl.semaphore_wait(barrier, n_tp - 1 + has_next.astype(jnp.int32) + has_prev.astype(jnp.int32))

    def columns(yy, zz):
        return pl.ds(pl.multiple_of((yy * 2 + zz) * PART, 128), PART)

    def relay(c):
        return pltpu.make_async_remote_copy(
            prev_ref.at[pl.ds(pl.multiple_of(c * ROWS, ROWS), ROWS)],
            xg.at[c, :, columns(y, z)],
            relay_send.at[c],
            relay_recv.at[c],
            device_id=next_dev,
            device_id_type=MESH,
        )

    def fresh(c):
        return pltpu.make_async_copy(
            fresh_ref.at[pl.ds(pl.multiple_of(c * ROWS, ROWS), ROWS)],
            xg.at[c, :, columns(y, z)],
            fresh_sem.at[c],
        )

    @pl.when(has_next)
    def _():
        for c in range(CHUNKS):
            relay(c).start()

    @pl.when(s == 0)
    def _():
        for c in range(CHUNKS):
            fresh(c).start()

    def gain_copy(q):
        return pltpu.make_async_remote_copy(
            gains.at[:, columns(y, z)],
            gains.at[:, columns(y, z)],
            gain_send.at[q - 1],
            gain_recv.at[q - 1],
            device_id=(s, (t + q) % n_tp),
            device_id_type=MESH,
        )

    gains[:, columns(y, z)] = jnp.broadcast_to(gain_ref[...].astype(F32), (8, PART))
    for q in range(1, n_tp):
        gain_copy(q).start()

    row_id = lax.broadcasted_iota(jnp.int32, (TILE, TILE), 0)
    col_id = lax.broadcasted_iota(jnp.int32, (TILE, TILE), 1)
    common = (row_id & col_id) & 127
    parity = common
    for shift in (4, 2, 1):
        parity = parity ^ (parity >> shift)
    same = (row_id >> 7) == (col_id >> 7)
    hada[...] = jnp.where(same, (1 - 2 * (parity & 1)).astype(F32), 0.0).astype(BF16)
    ones[...] = jnp.where(same, 1.0, 0.0).astype(BF16)

    def x_at(c, low, high, yy, zz):
        return xg.at[c, pl.ds(low, high - low), columns(yy, zz)]

    def r_at(c, low, high, yy, zz):
        return rot.at[c, pl.ds(low, high - low), columns(yy, zz)]

    def gathered(c, k):
        low, high, yy, zz, dev = (
            (0, ROWS, y, zo, dev_z),
            (0, ROWS, y, zo, dev_p),
            (0, ROWS, y, zo, dev_m),
            (LO, HI, y, zq, dev_p),
            (LO, HI, y, zq, dev_m),
            (0, HALF, ym, zo, dev_p),
            (HALF, ROWS, yp, zo, dev_m),
            (0, LO, ym, zo, dev_z),
            (HI, ROWS, ym, zo, dev_z),
            (0, LO, yp, zo, dev_z),
            (HI, ROWS, yp, zo, dev_z),
            (0, LO, yf, zo, dev_z),
            (HI, ROWS, yf, zo, dev_z),
            (LO, HALF, ym, zq, dev_p),
            (HALF, HI, yp, zq, dev_m),
        )[k]
        ref = x_at(c, low, high, yy, zz)
        return ref, ref, dev

    def summed(c, k):
        low, high, yy, zz, dev, dst = (
            (0, LO, yf, zb, dev_z, land1.at[c, pl.ds(0, LO)]),
            (HI, ROWS, yf, zb, dev_z, land1.at[c, pl.ds(HI, ROWS - HI)]),
            (LO, HALF, yf, zb, dev_p, land1.at[c, pl.ds(LO, HALF - LO)]),
            (HALF, HI, yf, zb, dev_m, land1.at[c, pl.ds(HALF, HI - HALF)]),
            (0, HALF, yf, z, dev_p, land2.at[c, pl.ds(0, HALF)]),
            (HALF, ROWS, yf, z, dev_m, land2.at[c, pl.ds(HALF, ROWS - HALF)]),
            (LO, HI, yp, zb, dev_p, land2.at[c, pl.ds(256, HI - LO)]),
            (LO, HI, ym, zb, dev_m, land2.at[c, pl.ds(400, HI - LO)]),
            (0, LO, yp, zb, dev_z, land2.at[c, pl.ds(544, LO)]),
            (HI, ROWS, yp, zb, dev_z, land2.at[c, pl.ds(592, ROWS - HI)]),
            (0, LO, ym, zb, dev_z, land2.at[c, pl.ds(656, LO)]),
            (HI, ROWS, ym, zb, dev_z, land2.at[c, pl.ds(704, ROWS - HI)]),
            (0, ROWS, yp, z, dev_p, land3.at[c, 0]),
            (0, ROWS, ym, z, dev_m, land3.at[c, 1]),
            (0, ROWS, y, zb, dev_z, land3.at[c, 2]),
        )[k - 15]
        return r_at(c, low, high, yy, zz), dst, dev

    def copy(c, k):
        src, dst, dev = gathered(c, k) if k < 15 else summed(c, k)
        return pltpu.make_async_remote_copy(
            src, dst, send.at[c, k], recv.at[c, k], device_id=dev, device_id_type=MESH
        )

    def start(c, *ks):
        for k in ks:
            copy(c, k).start()

    def arrive(c, *ks):
        for k in ks:
            copy(c, k).wait_recv()

    def gather_one(c):
        @pl.when(s == 0)
        def _():
            fresh(c).wait()

        @pl.when(has_prev)
        def _():
            relay(c).wait_recv()

        start(c, 0, 1, 2)

    def gather_two(c):
        arrive(c, 1)
        start(c, 5, 7, 8)
        arrive(c, 2)
        start(c, 6, 9, 10)
        arrive(c, 0)
        start(c, 3, 4)

    def gather_three(c):
        arrive(c, 5)
        start(c, 11)
        arrive(c, 6)
        start(c, 12)
        arrive(c, 3)
        start(c, 13)
        arrive(c, 4)
        start(c, 14)

    def turn_weights(first, count):
        def body(i, carry):
            at = first * 4 + i
            rows = pl.ds(pl.multiple_of((at % 4) * 256, 256), 256)
            cols = pl.ds(pl.multiple_of((at // 4) * TILE, TILE), TILE)
            turned = jnp.dot(wd[rows, cols], hada[...], preferred_element_type=F32)
            wd[rows, cols] = (turned * (1.0 / math.sqrt(128.0))).astype(BF16)
            return carry

        lax.fori_loop(0, count * 4, body, 0)

    def compute(c):
        arrive(c, 7, 8, 9, 10, 11, 12, 13, 14)

        def norm(i, carry):
            rows = pl.ds(pl.multiple_of(i * 16, 16), 16)
            wide = xg[c, rows, :].astype(F32)
            mean_square = jnp.sum(wide * wide, axis=1, keepdims=True) * (1.0 / D)
            nb[rows, :] = (wide * lax.rsqrt(mean_square + EPSILON) * gains[0:1, :]).astype(BF16)
            return carry

        lax.fori_loop(0, ROWS // 16, norm, 0)

        def into(i, carry):
            cols = pl.ds(pl.multiple_of(i * TILE, TILE), TILE)
            gate = jnp.dot(nb[...], wg[:, cols], preferred_element_type=F32)
            up = jnp.dot(nb[...], wu[:, cols], preferred_element_type=F32)
            hb[:, cols] = (gate / (1.0 + jnp.exp(-gate)) * up).astype(BF16)
            return carry

        lax.fori_loop(0, H_DEV // TILE, into, 0)

        def out_of(i, carry):
            cols = pl.ds(pl.multiple_of(i * TILE, TILE), TILE)
            turned = jnp.dot(hb[...], wd[:, cols], preferred_element_type=F32)
            squares = jnp.dot((turned * turned).astype(BF16), ones[...], preferred_element_type=F32)
            limit = CLIP_FACTOR * jnp.sqrt(squares * (1.0 / 128.0) + BLOCK_EPSILON)
            rot[c, :, cols] = jnp.clip(turned, -limit, limit).astype(BF16)
            return carry

        lax.fori_loop(0, D // TILE, out_of, 0)
        start(c, 15, 16, 17, 18)

    def add(c, low, high, yy, zz, *others):
        total = rot[c, low:high, columns(yy, zz)].astype(F32)
        for other in others:
            total = total + other.astype(F32)
        rot[c, low:high, columns(yy, zz)] = total.astype(BF16)

    def sum_two(c):
        arrive(c, 15, 16)
        add(c, 0, LO, yf, z, land1[c, 0:LO])
        add(c, HI, ROWS, yf, z, land1[c, HI:ROWS])
        start(c, 19, 20)
        arrive(c, 17)
        add(c, LO, HALF, yp, zb, land1[c, LO:HALF])
        start(c, 21)
        arrive(c, 18)
        add(c, HALF, HI, ym, zb, land1[c, HALF:HI])
        start(c, 22, 23, 24, 25, 26)

    def sum_three(c):
        arrive(c, 19, 23, 24)
        add(c, 0, LO, yp, z, land2[c, 0:LO], land2[c, 544:592])
        add(c, LO, HALF, yp, z, land2[c, LO:HALF])
        add(c, HI, ROWS, yp, z, land2[c, 592:656])
        start(c, 27)
        arrive(c, 20, 25, 26)
        add(c, 0, LO, ym, z, land2[c, 656:704])
        add(c, HALF, HI, ym, z, land2[c, HALF:HI])
        add(c, HI, ROWS, ym, z, land2[c, HI:ROWS], land2[c, 704:768])
        start(c, 28)
        arrive(c, 21, 22)
        add(c, LO, HI, y, zb, land2[c, 256:400], land2[c, 400:544])
        start(c, 29)

    def finish(c):
        arrive(c, 27, 28, 29)
        out_rows = pl.ds(pl.multiple_of(c * ROWS, ROWS), ROWS)
        for j in range(PART // 128):
            cols = pl.ds(pl.multiple_of((y * 2 + z) * PART + j * 128, 128), 128)
            here = slice(j * 128, (j + 1) * 128)
            total = rot[c, :, cols].astype(F32)
            for i in range(3):
                total = total + land3[c, i, :, here].astype(F32)
            high = total.astype(BF16)
            low = (total - high.astype(F32)).astype(BF16)
            table = hada[0:128, 0:128]
            update = jnp.dot(high, table, preferred_element_type=F32)
            update = update + jnp.dot(low, table, preferred_element_type=F32)
            incoming = xg[c, :, cols].astype(F32)
            out_ref[out_rows, here] = (incoming + update * (1.0 / math.sqrt(128.0))).astype(BF16)

    def step(i, carry):
        def stage(lag, work):
            @pl.when(jnp.logical_and(i >= lag, i < lag + CHUNKS))
            def _():
                work(i - lag)

        stage(0, gather_one)
        stage(1, gather_two)
        stage(2, gather_three)

        @pl.when(i == 0)
        def _():
            loads[0].wait()

        @pl.when(i < 3)
        def _():
            turn_weights(i * 4, 4)

        @pl.when(i == 3)
        def _():
            loads[1].wait()
            loads[2].wait()
            for q in range(1, n_tp):
                gain_copy(q).wait_recv()

        stage(3, compute)
        stage(4, sum_two)
        stage(5, sum_three)
        stage(6, finish)
        return carry

    lax.fori_loop(0, CHUNKS + 6, step, 0)

    def drain(c, carry):
        for k in range(COPIES):
            copy(c, k).wait_send()

        @pl.when(has_next)
        def _():
            relay(c).wait_send()

        return carry

    lax.fori_loop(0, CHUNKS, drain, 0)
    for q in range(1, n_tp):
        gain_copy(q).wait_send()


def local(fresh_input, previous_out, norm_gain, gate_weight, up_weight, down_weight):
    anywhere = pl.BlockSpec(memory_space=pl.ANY)
    vmem = pl.BlockSpec(memory_space=pltpu.VMEM)
    dma = pltpu.SemaphoreType.DMA
    return pl.pallas_call(
        kernel,
        out_shape=jax.ShapeDtypeStruct((TOK, PART), BF16),
        in_specs=[anywhere, anywhere, vmem, anywhere, anywhere, anywhere],
        out_specs=vmem,
        scratch_shapes=[
            pltpu.VMEM((CHUNKS, ROWS, D), BF16),
            pltpu.VMEM((D, H_DEV), BF16),
            pltpu.VMEM((D, H_DEV), BF16),
            pltpu.VMEM((H_DEV, D), BF16),
            pltpu.VMEM((CHUNKS, ROWS, D), BF16),
            pltpu.VMEM((CHUNKS, ROWS, PART), BF16),
            pltpu.VMEM((CHUNKS, 3 * ROWS, PART), BF16),
            pltpu.VMEM((CHUNKS, 3, ROWS, PART), BF16),
            pltpu.VMEM((ROWS, D), BF16),
            pltpu.VMEM((ROWS, H_DEV), BF16),
            pltpu.VMEM((8, D), F32),
            pltpu.VMEM((TILE, TILE), BF16),
            pltpu.VMEM((TILE, TILE), BF16),
            dma((3,)),
            dma((CHUNKS,)),
            dma((CHUNKS,)),
            dma((CHUNKS,)),
            dma((7,)),
            dma((7,)),
            dma((CHUNKS, COPIES)),
            dma((CHUNKS, COPIES)),
        ],
        compiler_params=pltpu.CompilerParams(
            collective_id=0, has_side_effects=True, vmem_limit_bytes=56 << 20
        ),
        cost_estimate=pl.CostEstimate(
            flops=2 * 3 * TOK * D * H_DEV, bytes_accessed=3 * 2 * D * H_DEV, transcendentals=TOK * H_DEV
        ),
        name="relayed_feed_forward",
    )(fresh_input, previous_out, norm_gain, gate_weight, up_weight, down_weight)


def solution(mesh):
    in_specs = (
        P(None, "tp"),
        P("section", "tp"),
        P("section", "tp"),
        P("section", None, "tp"),
        P("section", None, "tp"),
        P("section", "tp", None),
    )
    return jax.shard_map(local, mesh=mesh, in_specs=in_specs, out_specs=P("section", "tp"), check_vma=False)
```

```python
import math

import jax
import jax.numpy as jnp
from jax import lax
from jax.experimental import pallas as pl
from jax.experimental.pallas import tpu as pltpu
from jax.sharding import PartitionSpec as P

EPSILON = 1e-05
BLOCK_EPSILON = 1e-06
CLIP_FACTOR = 2.0

MESH = pl.DeviceIdType.MESH
F32 = jnp.float32
BF16 = jnp.bfloat16

TOK = 1024
D = 3072
H_DEV = 1024
PART = 384
ROWS = 256
CHUNKS = TOK // ROWS
TILE = 256
COPIES = 30
NORM_ROWS = 64

LO, HALF, HI = 48, 128, 192
S_LO, S_HI = 48, 192
MIDDLE = S_HI - S_LO
EDGE = ROWS - MIDDLE
EDGES = ROWS + 2 * MIDDLE


def kernel(
    fresh_ref, prev_ref, gain_ref, gate_ref, up_ref, down_ref, out_ref,
    xg, wg, wu, wd, rot, land1, land2, land3, nb, hb, gains, hada, ones,
    load_sem, fresh_sem, relay_send, relay_recv, gain_send, gain_recv, send, recv,
):
    s = lax.axis_index("section")
    t = lax.axis_index("tp")
    n_sections = lax.axis_size("section")
    n_tp = lax.axis_size("tp")
    y, z = t // 2, t % 2
    core = s % 2
    yp, ym, yf = (y + 1) % 4, (y + 3) % 4, (y + 2) % 4
    zb = 1 - z
    dev_p, dev_m, dev_z = (s, yp * 2 + z), (s, ym * 2 + z), (s, y * 2 + zb)
    has_next = s < n_sections - 1
    has_prev = s > 0
    next_dev = (jnp.minimum(s + 1, n_sections - 1), jnp.where(core == 0, t, y * 2 + zb))
    prev_dev = (jnp.maximum(s - 1, 0), jnp.where(core == 1, t, y * 2 + zb))
    zo = jnp.where(jnp.logical_or(core == 1, s == 0), z, zb)
    zq = 1 - zo

    loads = [
        pltpu.make_async_copy(src, dst, load_sem.at[i])
        for i, (src, dst) in enumerate(((down_ref.at[0], wd), (gate_ref.at[0], wg), (up_ref.at[0], wu)))
    ]
    for load in loads:
        load.start()

    barrier = pltpu.get_barrier_semaphore()
    for q in range(1, n_tp):
        pl.semaphore_signal(barrier, inc=1, device_id=(s, (t + q) % n_tp), device_id_type=MESH)

    @pl.when(has_next)
    def _():
        pl.semaphore_signal(barrier, inc=1, device_id=next_dev, device_id_type=MESH)

    @pl.when(has_prev)
    def _():
        pl.semaphore_signal(barrier, inc=1, device_id=prev_dev, device_id_type=MESH)

    pl.semaphore_wait(barrier, n_tp - 1 + has_next.astype(jnp.int32) + has_prev.astype(jnp.int32))

    def columns(yy, zz):
        return pl.ds(pl.multiple_of((yy * 2 + zz) * PART, 128), PART)

    def relay(c):
        return pltpu.make_async_remote_copy(
            prev_ref.at[pl.ds(pl.multiple_of(c * ROWS, ROWS), ROWS)],
            xg.at[c, :, columns(y, z)],
            relay_send.at[c],
            relay_recv.at[c],
            device_id=next_dev,
            device_id_type=MESH,
        )

    def fresh(c):
        return pltpu.make_async_copy(
            fresh_ref.at[pl.ds(pl.multiple_of(c * ROWS, ROWS), ROWS)],
            xg.at[c, :, columns(y, z)],
            fresh_sem.at[c],
        )

    @pl.when(has_next)
    def _():
        for c in range(CHUNKS):
            relay(c).start()

    @pl.when(s == 0)
    def _():
        for c in range(CHUNKS):
            fresh(c).start()

    def gain_copy(q):
        return pltpu.make_async_remote_copy(
            gains.at[:, columns(y, z)],
            gains.at[:, columns(y, z)],
            gain_send.at[q - 1],
            gain_recv.at[q - 1],
            device_id=(s, (t + q) % n_tp),
            device_id_type=MESH,
        )

    gains[:, columns(y, z)] = jnp.broadcast_to(gain_ref[...].astype(F32), (8, PART))
    for q in range(1, n_tp):
        gain_copy(q).start()

    row_id = lax.broadcasted_iota(jnp.int32, (TILE, TILE), 0)
    col_id = lax.broadcasted_iota(jnp.int32, (TILE, TILE), 1)
    common = (row_id & col_id) & 127
    parity = common
    for shift in (4, 2, 1):
        parity = parity ^ (parity >> shift)
    same = (row_id >> 7) == (col_id >> 7)
    hada[...] = jnp.where(same, (1 - 2 * (parity & 1)).astype(F32), 0.0).astype(BF16)
    ones[...] = jnp.where(same, 1.0, 0.0).astype(BF16)

    def x_at(c, low, high, yy, zz):
        return xg.at[c, pl.ds(low, high - low), columns(yy, zz)]

    def r_at(c, low, high, yy, zz):
        return rot.at[c, pl.ds(low, high - low), columns(yy, zz)]

    def gathered(c, k):
        low, high, yy, zz, dev = (
            (0, ROWS, y, zo, dev_z),
            (0, ROWS, y, zo, dev_p),
            (0, ROWS, y, zo, dev_m),
            (LO, HI, y, zq, dev_p),
            (LO, HI, y, zq, dev_m),
            (0, HALF, ym, zo, dev_p),
            (HALF, ROWS, yp, zo, dev_m),
            (0, LO, ym, zo, dev_z),
            (HI, ROWS, ym, zo, dev_z),
            (0, LO, yp, zo, dev_z),
            (HI, ROWS, yp, zo, dev_z),
            (0, LO, yf, zo, dev_z),
            (HI, ROWS, yf, zo, dev_z),
            (LO, HALF, ym, zq, dev_p),
            (HALF, HI, yp, zq, dev_m),
        )[k]
        ref = x_at(c, low, high, yy, zz)
        return ref, ref, dev

    def summed(c, k):
        low, high, yy, zz, dev, dst = (
            (0, S_LO, yf, zb, dev_z, land1.at[c, pl.ds(0, S_LO)]),
            (S_HI, ROWS, yf, zb, dev_z, land1.at[c, pl.ds(S_HI, ROWS - S_HI)]),
            (S_LO, HALF, yf, zb, dev_p, land1.at[c, pl.ds(S_LO, HALF - S_LO)]),
            (HALF, S_HI, yf, zb, dev_m, land1.at[c, pl.ds(HALF, S_HI - HALF)]),
            (0, HALF, yf, z, dev_p, land2.at[c, pl.ds(0, HALF)]),
            (HALF, ROWS, yf, z, dev_m, land2.at[c, pl.ds(HALF, ROWS - HALF)]),
            (S_LO, S_HI, yp, zb, dev_p, land2.at[c, pl.ds(ROWS, MIDDLE)]),
            (S_LO, S_HI, ym, zb, dev_m, land2.at[c, pl.ds(ROWS + MIDDLE, MIDDLE)]),
            (0, S_LO, yp, zb, dev_z, land2.at[c, pl.ds(EDGES, S_LO)]),
            (S_HI, ROWS, yp, zb, dev_z, land2.at[c, pl.ds(EDGES + S_LO, ROWS - S_HI)]),
            (0, S_LO, ym, zb, dev_z, land2.at[c, pl.ds(EDGES + EDGE, S_LO)]),
            (S_HI, ROWS, ym, zb, dev_z, land2.at[c, pl.ds(EDGES + EDGE + S_LO, ROWS - S_HI)]),
            (0, ROWS, yp, z, dev_p, land3.at[c, 0]),
            (0, ROWS, ym, z, dev_m, land3.at[c, 1]),
            (0, ROWS, y, zb, dev_z, land3.at[c, 2]),
        )[k - 15]
        return r_at(c, low, high, yy, zz), dst, dev

    def copy(c, k):
        src, dst, dev = gathered(c, k) if k < 15 else summed(c, k)
        return pltpu.make_async_remote_copy(
            src, dst, send.at[c, k], recv.at[c, k], device_id=dev, device_id_type=MESH
        )

    def start(c, *ks):
        for k in ks:
            copy(c, k).start()

    def arrive(c, *ks):
        for k in ks:
            copy(c, k).wait_recv()

    def gather_one(c):
        @pl.when(s == 0)
        def _():
            fresh(c).wait()

        @pl.when(has_prev)
        def _():
            relay(c).wait_recv()

        start(c, 0, 1, 2)

    def gather_two(c):
        arrive(c, 1)
        start(c, 5, 7, 8)
        arrive(c, 2)
        start(c, 6, 9, 10)
        arrive(c, 0)
        start(c, 3, 4)

    def gather_three(c):
        arrive(c, 5)
        start(c, 11)
        arrive(c, 6)
        start(c, 12)
        arrive(c, 3)
        start(c, 13)
        arrive(c, 4)
        start(c, 14)

    def turn_weights(first, count):
        def body(i, carry):
            at = first * 4 + i
            rows = pl.ds(pl.multiple_of((at % 4) * 256, 256), 256)
            cols = pl.ds(pl.multiple_of((at // 4) * TILE, TILE), TILE)
            turned = jnp.dot(wd[rows, cols], hada[...], preferred_element_type=F32)
            wd[rows, cols] = (turned * (1.0 / math.sqrt(128.0))).astype(BF16)
            return carry

        lax.fori_loop(0, count * 4, body, 0)

    def compute(c):
        arrive(c, 7, 8, 9, 10, 11, 12, 13, 14)

        def norm(i, carry):
            rows = pl.ds(pl.multiple_of(i * NORM_ROWS, NORM_ROWS), NORM_ROWS)
            wide = xg[c, rows, :].astype(F32)
            mean_square = jnp.sum(wide * wide, axis=1, keepdims=True) * (1.0 / D)
            nb[rows, :] = (wide * lax.rsqrt(mean_square + EPSILON) * gains[0:1, :]).astype(BF16)
            return carry

        lax.fori_loop(0, ROWS // NORM_ROWS, norm, 0)
        gate = jnp.dot(nb[...], wg[...], preferred_element_type=F32)
        up = jnp.dot(nb[...], wu[...], preferred_element_type=F32)
        hb[...] = (gate / (1.0 + jnp.exp(-gate)) * up).astype(BF16)
        term = jnp.dot(hb[...], wd[...], preferred_element_type=F32)
        for j in range(0, D, TILE):
            turned = term[:, j : j + TILE]
            squares = jnp.dot((turned * turned).astype(BF16), ones[...], preferred_element_type=F32)
            fourfold = squares * (CLIP_FACTOR**2 / 128.0) + CLIP_FACTOR**2 * BLOCK_EPSILON
            limit = fourfold * lax.rsqrt(fourfold)
            rot[c, :, j : j + TILE] = jnp.minimum(jnp.maximum(turned, -limit), limit).astype(BF16)
        start(c, 15, 16, 17, 18)

    def add(c, low, high, yy, zz, *others):
        total = rot[c, low:high, columns(yy, zz)].astype(F32)
        for other in others:
            total = total + other.astype(F32)
        rot[c, low:high, columns(yy, zz)] = total.astype(BF16)

    def sum_two(c):
        arrive(c, 15, 16)
        add(c, 0, S_LO, yf, z, land1[c, 0:S_LO])
        add(c, S_HI, ROWS, yf, z, land1[c, S_HI:ROWS])
        start(c, 19, 20)
        arrive(c, 17)
        add(c, S_LO, HALF, yp, zb, land1[c, S_LO:HALF])
        start(c, 21)
        arrive(c, 18)
        add(c, HALF, S_HI, ym, zb, land1[c, HALF:S_HI])
        start(c, 22, 23, 24, 25, 26)

    def sum_three(c):
        arrive(c, 19, 23, 24)
        add(c, 0, S_LO, yp, z, land2[c, 0:S_LO], land2[c, EDGES : EDGES + S_LO])
        add(c, S_LO, HALF, yp, z, land2[c, S_LO:HALF])
        add(c, S_HI, ROWS, yp, z, land2[c, EDGES + S_LO : EDGES + EDGE])
        start(c, 27)
        arrive(c, 20, 25, 26)
        add(c, 0, S_LO, ym, z, land2[c, EDGES + EDGE : EDGES + EDGE + S_LO])
        add(c, HALF, S_HI, ym, z, land2[c, HALF:S_HI])
        add(c, S_HI, ROWS, ym, z, land2[c, S_HI:ROWS], land2[c, EDGES + EDGE + S_LO : EDGES + 2 * EDGE])
        start(c, 28)
        arrive(c, 21, 22)
        add(c, S_LO, S_HI, y, zb, land2[c, ROWS : ROWS + MIDDLE], land2[c, ROWS + MIDDLE : EDGES])
        start(c, 29)

    def finish(c):
        arrive(c, 27, 28, 29)
        out_rows = pl.ds(pl.multiple_of(c * ROWS, ROWS), ROWS)
        for j in range(PART // 128):
            cols = pl.ds(pl.multiple_of((y * 2 + z) * PART + j * 128, 128), 128)
            here = slice(j * 128, (j + 1) * 128)
            total = rot[c, :, cols].astype(F32)
            for i in range(3):
                total = total + land3[c, i, :, here].astype(F32)
            high = total.astype(BF16)
            low = (total - high.astype(F32)).astype(BF16)
            table = hada[0:128, 0:128]
            update = jnp.dot(high, table, preferred_element_type=F32)
            update = update + jnp.dot(low, table, preferred_element_type=F32)
            incoming = xg[c, :, cols].astype(F32)
            out_ref[out_rows, here] = (incoming + update * (1.0 / math.sqrt(128.0))).astype(BF16)

    def step(i, carry):
        def stage(lag, work):
            @pl.when(jnp.logical_and(i >= lag, i < lag + CHUNKS))
            def _():
                work(i - lag)

        stage(0, gather_one)
        stage(1, gather_two)
        stage(2, gather_three)

        @pl.when(i == 0)
        def _():
            loads[0].wait()

        @pl.when(i < 3)
        def _():
            turn_weights(i * 4, 4)

        @pl.when(i == 3)
        def _():
            loads[1].wait()
            loads[2].wait()
            for q in range(1, n_tp):
                gain_copy(q).wait_recv()

        stage(3, compute)
        stage(4, sum_two)
        stage(5, sum_three)
        stage(6, finish)
        return carry

    lax.fori_loop(0, CHUNKS + 6, step, 0)

    def drain(c, carry):
        for k in range(COPIES):
            copy(c, k).wait_send()

        @pl.when(has_next)
        def _():
            relay(c).wait_send()

        return carry

    lax.fori_loop(0, CHUNKS, drain, 0)
    for q in range(1, n_tp):
        gain_copy(q).wait_send()


def local(fresh_input, previous_out, norm_gain, gate_weight, up_weight, down_weight):
    anywhere = pl.BlockSpec(memory_space=pl.ANY)
    vmem = pl.BlockSpec(memory_space=pltpu.VMEM)
    dma = pltpu.SemaphoreType.DMA
    return pl.pallas_call(
        kernel,
        out_shape=jax.ShapeDtypeStruct((TOK, PART), BF16),
        in_specs=[anywhere, anywhere, vmem, anywhere, anywhere, anywhere],
        out_specs=vmem,
        scratch_shapes=[
            pltpu.VMEM((CHUNKS, ROWS, D), BF16),
            pltpu.VMEM((D, H_DEV), BF16),
            pltpu.VMEM((D, H_DEV), BF16),
            pltpu.VMEM((H_DEV, D), BF16),
            pltpu.VMEM((CHUNKS, ROWS, D), BF16),
            pltpu.VMEM((CHUNKS, ROWS, PART), BF16),
            pltpu.VMEM((CHUNKS, 3 * ROWS, PART), BF16),
            pltpu.VMEM((CHUNKS, 3, ROWS, PART), BF16),
            pltpu.VMEM((ROWS, D), BF16),
            pltpu.VMEM((ROWS, H_DEV), BF16),
            pltpu.VMEM((8, D), F32),
            pltpu.VMEM((TILE, TILE), BF16),
            pltpu.VMEM((TILE, TILE), BF16),
            dma((3,)),
            dma((CHUNKS,)),
            dma((CHUNKS,)),
            dma((CHUNKS,)),
            dma((7,)),
            dma((7,)),
            dma((CHUNKS, COPIES)),
            dma((CHUNKS, COPIES)),
        ],
        compiler_params=pltpu.CompilerParams(
            collective_id=0, has_side_effects=True, vmem_limit_bytes=56 << 20
        ),
        cost_estimate=pl.CostEstimate(
            flops=2 * 3 * TOK * D * H_DEV, bytes_accessed=3 * 2 * D * H_DEV, transcendentals=TOK * H_DEV
        ),
        name="relayed_feed_forward",
    )(fresh_input, previous_out, norm_gain, gate_weight, up_weight, down_weight)


def solution(mesh):
    in_specs = (
        P(None, "tp"),
        P("section", "tp"),
        P("section", "tp"),
        P("section", None, "tp"),
        P("section", None, "tp"),
        P("section", "tp", None),
    )
    return jax.shard_map(local, mesh=mesh, in_specs=in_specs, out_specs=P("section", "tp"), check_vma=False)
```

```python
import math

import jax
import jax.numpy as jnp
from jax import lax
from jax.experimental import pallas as pl
from jax.experimental.pallas import tpu as pltpu
from jax.sharding import PartitionSpec as P

EPSILON = 1e-05
BLOCK_EPSILON = 1e-06
CLIP_FACTOR = 2.0

MESH = pl.DeviceIdType.MESH
F32 = jnp.float32
BF16 = jnp.bfloat16

TOK = 1024
D = 3072
H_DEV = 1024
PART = 384
ROWS = 256
CHUNKS = TOK // ROWS
TILE = 256
COPIES = 30
PIECES = 4
PIECE = ROWS // PIECES
SLOTS = PIECES - 1 + CHUNKS
NORM_ROWS = 64

LO, HALF, HI = 48, 128, 192
S_LO, S_HALF, S_HI = 64, 128, 208
MIDDLE = S_HI - S_LO
EDGE = ROWS - MIDDLE
EDGES = ROWS + 2 * MIDDLE


def kernel(
    fresh_ref, prev_ref, gain_ref, gate_ref, up_ref, down_ref, out_ref,
    xg, wg, wu, wd, rot, done, land1, land2, land3, nb, hb, gains, hada, ones,
    out_sem, load_sem, fresh_sem, relay_send, relay_recv, first_send, first_recv, gain_send, gain_recv, send, recv,
):
    s = lax.axis_index("section")
    t = lax.axis_index("tp")
    n_sections = lax.axis_size("section")
    n_tp = lax.axis_size("tp")
    y, z = t // 2, t % 2
    core = s % 2
    yp, ym, yf = (y + 1) % 4, (y + 3) % 4, (y + 2) % 4
    zb = 1 - z
    dev_p, dev_m, dev_z = (s, yp * 2 + z), (s, ym * 2 + z), (s, y * 2 + zb)
    has_next = s < n_sections - 1
    has_prev = s > 0
    next_dev = (jnp.minimum(s + 1, n_sections - 1), jnp.where(core == 0, t, y * 2 + zb))
    prev_dev = (jnp.maximum(s - 1, 0), jnp.where(core == 1, t, y * 2 + zb))
    zo = jnp.where(jnp.logical_or(core == 1, s == 0), z, zb)
    zq = 1 - zo

    loads = [
        pltpu.make_async_copy(src, dst, load_sem.at[i])
        for i, (src, dst) in enumerate(((down_ref.at[0], wd), (gate_ref.at[0], wg), (up_ref.at[0], wu)))
    ]
    for load in loads:
        load.start()

    barrier = pltpu.get_barrier_semaphore()
    for q in range(1, n_tp):
        pl.semaphore_signal(barrier, inc=1, device_id=(s, (t + q) % n_tp), device_id_type=MESH)

    @pl.when(has_next)
    def _():
        pl.semaphore_signal(barrier, inc=1, device_id=next_dev, device_id_type=MESH)

    @pl.when(has_prev)
    def _():
        pl.semaphore_signal(barrier, inc=1, device_id=prev_dev, device_id_type=MESH)

    pl.semaphore_wait(barrier, n_tp - 1 + has_next.astype(jnp.int32) + has_prev.astype(jnp.int32))

    def columns(yy, zz):
        return pl.ds(pl.multiple_of((yy * 2 + zz) * PART, 128), PART)

    def source(ref, slot):
        if isinstance(slot, int) and slot < PIECES:
            return ref.at[pl.ds(slot * PIECE, PIECE)], xg.at[0, pl.ds(slot * PIECE, PIECE), columns(y, z)]
        c = slot - (PIECES - 1)
        return ref.at[pl.ds(pl.multiple_of(c * ROWS, ROWS), ROWS)], xg.at[c, :, columns(y, z)]

    def relay(slot):
        src, dst = source(prev_ref, slot)
        return pltpu.make_async_remote_copy(
            src, dst, relay_send.at[slot], relay_recv.at[slot], device_id=next_dev, device_id_type=MESH
        )

    def fresh(slot):
        src, dst = source(fresh_ref, slot)
        return pltpu.make_async_copy(src, dst, fresh_sem.at[slot])

    @pl.when(has_next)
    def _():
        for slot in range(SLOTS):
            relay(slot).start()

    @pl.when(s == 0)
    def _():
        for slot in range(SLOTS):
            fresh(slot).start()

    def incoming_rows(slot):
        @pl.when(s == 0)
        def _():
            fresh(slot).wait()

        @pl.when(has_prev)
        def _():
            relay(slot).wait_recv()

    def first(p, d):
        ref = xg.at[0, pl.ds(p * PIECE, PIECE), columns(y, zo)]
        return pltpu.make_async_remote_copy(
            ref, ref, first_send.at[p, d], first_recv.at[p, d], device_id=(dev_z, dev_p, dev_m)[d], device_id_type=MESH
        )

    for p in range(PIECES):
        incoming_rows(p)
        for d in range(3):
            first(p, d).start()

    def gain_copy(q):
        return pltpu.make_async_remote_copy(
            gains.at[pl.ds(0, 1), columns(y, z)],
            gains.at[pl.ds(0, 1), columns(y, z)],
            gain_send.at[q - 1],
            gain_recv.at[q - 1],
            device_id=(s, (t + q) % n_tp),
            device_id_type=MESH,
        )

    gains[0:1, columns(y, z)] = gain_ref[...].astype(F32)
    for q in range(1, n_tp):
        gain_copy(q).start()

    row_id = lax.broadcasted_iota(jnp.int32, (TILE, TILE), 0)
    col_id = lax.broadcasted_iota(jnp.int32, (TILE, TILE), 1)
    common = (row_id & col_id) & 127
    parity = common
    for shift in (4, 2, 1):
        parity = parity ^ (parity >> shift)
    same = (row_id >> 7) == (col_id >> 7)
    hada[...] = jnp.where(same, (1 - 2 * (parity & 1)).astype(F32), 0.0).astype(BF16)
    ones[...] = jnp.where(same, 1.0, 0.0).astype(BF16)

    def x_at(c, low, high, yy, zz):
        return xg.at[c, pl.ds(low, high - low), columns(yy, zz)]

    def r_at(c, low, high, yy, zz):
        return rot.at[c, pl.ds(low, high - low), columns(yy, zz)]

    def gathered(c, k):
        low, high, yy, zz, dev = (
            (0, ROWS, y, zo, dev_z),
            (0, ROWS, y, zo, dev_p),
            (0, ROWS, y, zo, dev_m),
            (LO, HI, y, zq, dev_p),
            (LO, HI, y, zq, dev_m),
            (0, HALF, ym, zo, dev_p),
            (HALF, ROWS, yp, zo, dev_m),
            (0, LO, ym, zo, dev_z),
            (HI, ROWS, ym, zo, dev_z),
            (0, LO, yp, zo, dev_z),
            (HI, ROWS, yp, zo, dev_z),
            (0, LO, yf, zo, dev_z),
            (HI, ROWS, yf, zo, dev_z),
            (LO, HALF, ym, zq, dev_p),
            (HALF, HI, yp, zq, dev_m),
        )[k]
        ref = x_at(c, low, high, yy, zz)
        return ref, ref, dev

    def summed(c, k):
        low, high, yy, zz, dev, dst = (
            (0, S_LO, yf, zb, dev_z, land1.at[c, pl.ds(0, S_LO)]),
            (S_HI, ROWS, yf, zb, dev_z, land1.at[c, pl.ds(S_HI, ROWS - S_HI)]),
            (S_LO, S_HALF, yf, zb, dev_p, land1.at[c, pl.ds(S_LO, S_HALF - S_LO)]),
            (S_HALF, S_HI, yf, zb, dev_m, land1.at[c, pl.ds(S_HALF, S_HI - S_HALF)]),
            (0, S_HALF, yf, z, dev_p, land2.at[c, pl.ds(0, S_HALF)]),
            (S_HALF, ROWS, yf, z, dev_m, land2.at[c, pl.ds(S_HALF, ROWS - S_HALF)]),
            (S_LO, S_HI, yp, zb, dev_p, land2.at[c, pl.ds(ROWS, MIDDLE)]),
            (S_LO, S_HI, ym, zb, dev_m, land2.at[c, pl.ds(ROWS + MIDDLE, MIDDLE)]),
            (0, S_LO, yp, zb, dev_z, land2.at[c, pl.ds(EDGES, S_LO)]),
            (S_HI, ROWS, yp, zb, dev_z, land2.at[c, pl.ds(EDGES + S_LO, ROWS - S_HI)]),
            (0, S_LO, ym, zb, dev_z, land2.at[c, pl.ds(EDGES + EDGE, S_LO)]),
            (S_HI, ROWS, ym, zb, dev_z, land2.at[c, pl.ds(EDGES + EDGE + S_LO, ROWS - S_HI)]),
            (0, ROWS, yp, z, dev_p, land3.at[c, 0]),
            (0, ROWS, ym, z, dev_m, land3.at[c, 1]),
            (0, ROWS, y, zb, dev_z, land3.at[c, 2]),
        )[k - 15]
        return r_at(c, low, high, yy, zz), dst, dev

    def copy(c, k):
        src, dst, dev = gathered(c, k) if k < 15 else summed(c, k)
        return pltpu.make_async_remote_copy(
            src, dst, send.at[c, k], recv.at[c, k], device_id=dev, device_id_type=MESH
        )

    def start(c, *ks):
        for k in ks:
            copy(c, k).start()

    def arrive(c, *ks):
        for k in ks:
            copy(c, k).wait_recv()

    def gather_one(c):
        @pl.when(c > 0)
        def _():
            incoming_rows(PIECES - 1 + c)
            start(c, 0, 1, 2)

    def arrive_own(c, d):
        @pl.when(c == 0)
        def _():
            for p in range(PIECES):
                first(p, d).wait_recv()

        @pl.when(c > 0)
        def _():
            arrive(c, d)

    def gather_two(c):
        arrive_own(c, 1)
        start(c, 5, 7, 8)
        arrive_own(c, 2)
        start(c, 6, 9, 10)
        arrive_own(c, 0)
        start(c, 3, 4)

    def gather_three(c):
        arrive(c, 5)
        start(c, 11)
        arrive(c, 6)
        start(c, 12)
        arrive(c, 3)
        start(c, 13)
        arrive(c, 4)
        start(c, 14)

    def turn_weights(first, count):
        def body(i, carry):
            cols = pl.ds(pl.multiple_of((first + i) * TILE, TILE), TILE)
            turned = jnp.dot(wd[:, cols], hada[...], preferred_element_type=F32)
            wd[:, cols] = (turned * (1.0 / math.sqrt(128.0))).astype(BF16)
            return carry

        lax.fori_loop(0, count, body, 0)

    def compute(c):
        arrive(c, 7, 8, 9, 10, 11, 12, 13, 14)

        def norm(i, carry):
            rows = pl.ds(pl.multiple_of(i * NORM_ROWS, NORM_ROWS), NORM_ROWS)
            wide = xg[c, rows, :].astype(F32)
            mean_square = jnp.sum(wide * wide, axis=1, keepdims=True) * (1.0 / D)
            nb[rows, :] = (wide * lax.rsqrt(mean_square + EPSILON) * gains[0:1, :]).astype(BF16)
            return carry

        lax.fori_loop(0, ROWS // NORM_ROWS, norm, 0)
        gate = jnp.dot(nb[...], wg[...], preferred_element_type=F32)
        up = jnp.dot(nb[...], wu[...], preferred_element_type=F32)
        hb[...] = (gate / (1.0 + jnp.exp(-gate)) * up).astype(BF16)
    def compute_out(c):
        term = jnp.dot(hb[...], wd[...], preferred_element_type=F32)
        for j in range(0, D, TILE):
            turned = term[:, j : j + TILE]
            squares = jnp.dot((turned * turned).astype(BF16), ones[...], preferred_element_type=F32)
            fourfold = squares * (CLIP_FACTOR**2 / 128.0) + CLIP_FACTOR**2 * BLOCK_EPSILON
            limit = fourfold * lax.rsqrt(fourfold)
            rot[c, :, j : j + TILE] = jnp.minimum(jnp.maximum(turned, -limit), limit).astype(BF16)
        start(c, 15, 16, 17, 18)

    def add(c, low, high, yy, zz, *others):
        total = rot[c, low:high, columns(yy, zz)].astype(F32)
        for other in others:
            total = total + other.astype(F32)
        rot[c, low:high, columns(yy, zz)] = total.astype(BF16)

    def sum_two(c):
        arrive(c, 15, 16)
        add(c, 0, S_LO, yf, z, land1[c, 0:S_LO])
        add(c, S_HI, ROWS, yf, z, land1[c, S_HI:ROWS])
        start(c, 19, 20)
        arrive(c, 17)
        add(c, S_LO, S_HALF, yp, zb, land1[c, S_LO:S_HALF])
        start(c, 21)
        arrive(c, 18)
        add(c, S_HALF, S_HI, ym, zb, land1[c, S_HALF:S_HI])
        start(c, 22, 23, 24, 25, 26)

    def sum_three(c):
        arrive(c, 19, 23, 24)
        add(c, 0, S_LO, yp, z, land2[c, 0:S_LO], land2[c, EDGES : EDGES + S_LO])
        add(c, S_LO, S_HALF, yp, z, land2[c, S_LO:S_HALF])
        add(c, S_HI, ROWS, yp, z, land2[c, EDGES + S_LO : EDGES + EDGE])
        start(c, 27)
        arrive(c, 20, 25, 26)
        add(c, 0, S_LO, ym, z, land2[c, EDGES + EDGE : EDGES + EDGE + S_LO])
        add(c, S_HALF, S_HI, ym, z, land2[c, S_HALF:S_HI])
        add(c, S_HI, ROWS, ym, z, land2[c, S_HI:ROWS], land2[c, EDGES + EDGE + S_LO : EDGES + 2 * EDGE])
        start(c, 28)
        arrive(c, 21, 22)
        add(c, S_LO, S_HI, y, zb, land2[c, ROWS : ROWS + MIDDLE], land2[c, ROWS + MIDDLE : EDGES])
        start(c, 29)

    def finish(c):
        arrive(c, 27, 28, 29)
        out_rows = pl.ds(pl.multiple_of(c * ROWS, ROWS), ROWS)
        for j in range(PART // 128):
            cols = pl.ds(pl.multiple_of((y * 2 + z) * PART + j * 128, 128), 128)
            here = slice(j * 128, (j + 1) * 128)
            total = rot[c, :, cols].astype(F32)
            for i in range(3):
                total = total + land3[c, i, :, here].astype(F32)
            high = total.astype(BF16)
            low = (total - high.astype(F32)).astype(BF16)
            table = hada[0:128, 0:128]
            update = jnp.dot(high, table, preferred_element_type=F32)
            update = update + jnp.dot(low, table, preferred_element_type=F32)
            incoming = xg[c, :, cols].astype(F32)
            done[out_rows, here] = (incoming + update * (1.0 / math.sqrt(128.0))).astype(BF16)

        written(c).start()

    def written(c):
        rows = pl.ds(pl.multiple_of(c * ROWS, ROWS), ROWS)
        return pltpu.make_async_copy(done.at[rows], out_ref.at[rows], out_sem.at[c])

    def step(i, carry):
        def stage(lag, work):
            @pl.when(jnp.logical_and(i >= lag, i < lag + CHUNKS))
            def _():
                work(i - lag)

        stage(0, gather_one)
        stage(1, gather_two)
        stage(2, gather_three)

        @pl.when(i == 0)
        def _():
            loads[0].wait()

        @pl.when(i < 3)
        def _():
            turn_weights(i * 4, 4)

        @pl.when(i == 3)
        def _():
            loads[1].wait()
            loads[2].wait()
            for q in range(1, n_tp):
                gain_copy(q).wait_recv()

        stage(3, compute)
        stage(4, sum_two)
        stage(3, compute_out)
        stage(5, sum_three)
        stage(6, finish)
        return carry

    lax.fori_loop(0, CHUNKS + 6, step, 0)

    def drain(c, carry):
        @pl.when(c > 0)
        def _():
            for k in range(3):
                copy(c, k).wait_send()

        for k in range(3, COPIES):
            copy(c, k).wait_send()

        written(c).wait()

        return carry

    lax.fori_loop(0, CHUNKS, drain, 0)
    for p in range(PIECES):
        for d in range(3):
            first(p, d).wait_send()

    @pl.when(has_next)
    def _():
        for slot in range(SLOTS):
            relay(slot).wait_send()

    for q in range(1, n_tp):
        gain_copy(q).wait_send()


def local(fresh_input, previous_out, norm_gain, gate_weight, up_weight, down_weight):
    anywhere = pl.BlockSpec(memory_space=pl.ANY)
    vmem = pl.BlockSpec(memory_space=pltpu.VMEM)
    dma = pltpu.SemaphoreType.DMA
    return pl.pallas_call(
        kernel,
        out_shape=jax.ShapeDtypeStruct((TOK, PART), BF16),
        in_specs=[anywhere, anywhere, vmem, anywhere, anywhere, anywhere],
        out_specs=anywhere,
        scratch_shapes=[
            pltpu.VMEM((CHUNKS, ROWS, D), BF16),
            pltpu.VMEM((D, H_DEV), BF16),
            pltpu.VMEM((D, H_DEV), BF16),
            pltpu.VMEM((H_DEV, D), BF16),
            pltpu.VMEM((CHUNKS, ROWS, D), BF16),
            pltpu.VMEM((TOK, PART), BF16),
            pltpu.VMEM((CHUNKS, ROWS, PART), BF16),
            pltpu.VMEM((CHUNKS, 3 * ROWS, PART), BF16),
            pltpu.VMEM((CHUNKS, 3, ROWS, PART), BF16),
            pltpu.VMEM((ROWS, D), BF16),
            pltpu.VMEM((ROWS, H_DEV), BF16),
            pltpu.VMEM((8, D), F32),
            pltpu.VMEM((TILE, TILE), BF16),
            pltpu.VMEM((TILE, TILE), BF16),
            dma((CHUNKS,)),
            dma((3,)),
            dma((SLOTS,)),
            dma((SLOTS,)),
            dma((SLOTS,)),
            dma((PIECES, 3)),
            dma((PIECES, 3)),
            dma((7,)),
            dma((7,)),
            dma((CHUNKS, COPIES)),
            dma((CHUNKS, COPIES)),
        ],
        compiler_params=pltpu.CompilerParams(
            collective_id=0, has_side_effects=True, vmem_limit_bytes=56 << 20
        ),
        cost_estimate=pl.CostEstimate(
            flops=2 * 3 * TOK * D * H_DEV, bytes_accessed=3 * 2 * D * H_DEV, transcendentals=TOK * H_DEV
        ),
        name="relayed_feed_forward",
    )(fresh_input, previous_out, norm_gain, gate_weight, up_weight, down_weight)


def solution(mesh):
    in_specs = (
        P(None, "tp"),
        P("section", "tp"),
        P("section", "tp"),
        P("section", None, "tp"),
        P("section", None, "tp"),
        P("section", "tp", None),
    )
    return jax.shard_map(local, mesh=mesh, in_specs=in_specs, out_specs=P("section", "tp"), check_vma=False)
```

```python
import math

import jax
import jax.numpy as jnp
from jax import lax
from jax.experimental import pallas as pl
from jax.experimental.pallas import tpu as pltpu
from jax.sharding import PartitionSpec as P

EPSILON = 1e-05
BLOCK_EPSILON = 1e-06
CLIP_FACTOR = 2.0

MESH = pl.DeviceIdType.MESH
F32 = jnp.float32
BF16 = jnp.bfloat16

TOK = 1024
D = 3072
H_DEV = 1024
N_TP = 8
PART = 384
ROWS = 256
CHUNKS = TOK // ROWS
TILE = 256
NORM_ROWS = 64

LO, HALF, HI = 48, 128, 192
S_LO, S_HALF, S_HI = 64, 128, 208
MIDDLE = S_HI - S_LO
EDGE = ROWS - MIDDLE
EDGES = ROWS + 2 * MIDDLE

GROUPS = (
    (0,), (1,), (2,), (3, 4), (5, 6), (7, 8, 9, 10, 11, 12, 13, 14),
    (15, 16), (17, 18), (19, 23, 24), (20, 25, 26), (21, 22), (27, 28, 29),
)
GROUP_OF = {k: group for group, ks in enumerate(GROUPS) for k in ks}
GROUP_ROWS = (
    ROWS, ROWS, ROWS, 2 * (HI - LO), ROWS, 3 * (ROWS - HI + LO) + HI - LO,
    EDGE, MIDDLE, S_HALF + EDGE, ROWS - S_HALF + EDGE, 2 * MIDDLE, 3 * ROWS,
)


def kernel(
    fresh_ref, prev_ref, gain_ref, gate_ref, up_ref, down_ref, out_ref,
    xg, wg, wu, wd, rot, land1, land2, land3, nb, hb, gains, hada, ones, gain,
    gain_sem, load_sem, relayed, gained, sent, landed,
):
    s = lax.axis_index("section")
    t = lax.axis_index("tp")
    n_sections = lax.axis_size("section")
    n_tp = lax.axis_size("tp")
    y, z = t // 2, t % 2
    core = s % 2
    yp, ym, yf = (y + 1) % 4, (y + 3) % 4, (y + 2) % 4
    zb = 1 - z
    dev_p, dev_m, dev_z = (s, yp * 2 + z), (s, ym * 2 + z), (s, y * 2 + zb)
    has_next = s < n_sections - 1
    has_prev = s > 0
    next_dev = (jnp.minimum(s + 1, n_sections - 1), jnp.where(core == 0, t, y * 2 + zb))
    prev_dev = (jnp.maximum(s - 1, 0), jnp.where(core == 1, t, y * 2 + zb))
    zo = jnp.where(jnp.logical_or(core == 1, s == 0), z, zb)
    zq = 1 - zo

    loads = [
        pltpu.make_async_copy(src, dst, load_sem.at[i])
        for i, (src, dst) in enumerate(((down_ref.at[0], wd), (gate_ref.at[0], wg), (up_ref.at[0], wu)))
    ]
    gain_load = pltpu.make_async_copy(gain_ref, gain, gain_sem)
    gain_load.start()
    for load in loads:
        load.start()

    barrier = pltpu.get_barrier_semaphore()
    for q in range(1, n_tp):
        pl.semaphore_signal(barrier, inc=1, device_id=(s, (t + q) % n_tp), device_id_type=MESH)

    @pl.when(has_next)
    def _():
        pl.semaphore_signal(barrier, inc=1, device_id=next_dev, device_id_type=MESH)

    @pl.when(has_prev)
    def _():
        pl.semaphore_signal(barrier, inc=1, device_id=prev_dev, device_id_type=MESH)

    pl.semaphore_wait(barrier, n_tp - 1 + has_next.astype(jnp.int32) + has_prev.astype(jnp.int32))

    def columns(yy, zz):
        return pl.ds(pl.multiple_of((yy * 2 + zz) * PART, 128), PART)

    def chunk_rows(c):
        return pl.ds(pl.multiple_of(c * ROWS, ROWS), ROWS)

    def relay(c):
        return pltpu.make_async_remote_copy(
            prev_ref.at[chunk_rows(c)],
            xg.at[c, :, columns(y, z)],
            sent.at[2],
            relayed.at[c],
            device_id=next_dev,
            device_id_type=MESH,
        )

    @pl.when(has_next)
    def _():
        for c in range(CHUNKS):
            relay(c).start()

    @pl.when(s == 0)
    def _():
        for c in range(CHUNKS):
            pltpu.make_async_copy(
                fresh_ref.at[chunk_rows(c)], xg.at[c, :, columns(y, z)], relayed.at[c]
            ).start()

    def gain_copy(cols, dev):
        row = gains.at[pl.ds(0, 1), cols]
        return pltpu.make_async_remote_copy(
            row, row, sent.at[3], gained, device_id=dev, device_id_type=MESH
        )

    all_gains = gain_copy(pl.ds(0, (N_TP - 1) * PART), dev_z)

    gain_load.wait()
    gains[0:1, columns(y, z)] = gain[...].astype(F32)
    for q in range(1, n_tp):
        gain_copy(columns(y, z), (s, (t + q) % n_tp)).start()

    row_id = lax.broadcasted_iota(jnp.int32, (TILE, TILE), 0)
    col_id = lax.broadcasted_iota(jnp.int32, (TILE, TILE), 1)
    common = (row_id & col_id) & 127
    parity = common
    for shift in (4, 2, 1):
        parity = parity ^ (parity >> shift)
    same = (row_id >> 7) == (col_id >> 7)
    hada[...] = jnp.where(same, (1 - 2 * (parity & 1)).astype(F32), 0.0).astype(BF16)
    ones[...] = jnp.where(same, 1.0, 0.0).astype(BF16)

    def x_at(c, low, high, yy, zz):
        return xg.at[c, pl.ds(low, high - low), columns(yy, zz)]

    def r_at(c, low, high, yy, zz):
        return rot.at[c, pl.ds(low, high - low), columns(yy, zz)]

    def gathered(c, k):
        low, high, yy, zz, dev = (
            (0, ROWS, y, zo, dev_z),
            (0, ROWS, y, zo, dev_p),
            (0, ROWS, y, zo, dev_m),
            (LO, HI, y, zq, dev_p),
            (LO, HI, y, zq, dev_m),
            (0, HALF, ym, zo, dev_p),
            (HALF, ROWS, yp, zo, dev_m),
            (0, LO, ym, zo, dev_z),
            (HI, ROWS, ym, zo, dev_z),
            (0, LO, yp, zo, dev_z),
            (HI, ROWS, yp, zo, dev_z),
            (0, LO, yf, zo, dev_z),
            (HI, ROWS, yf, zo, dev_z),
            (LO, HALF, ym, zq, dev_p),
            (HALF, HI, yp, zq, dev_m),
        )[k]
        ref = x_at(c, low, high, yy, zz)
        return ref, ref, dev

    def summed(c, k):
        low, high, yy, zz, dev, dst = (
            (0, S_LO, yf, zb, dev_z, land1.at[c, pl.ds(0, S_LO)]),
            (S_HI, ROWS, yf, zb, dev_z, land1.at[c, pl.ds(S_HI, ROWS - S_HI)]),
            (S_LO, S_HALF, yf, zb, dev_p, land1.at[c, pl.ds(S_LO, S_HALF - S_LO)]),
            (S_HALF, S_HI, yf, zb, dev_m, land1.at[c, pl.ds(S_HALF, S_HI - S_HALF)]),
            (0, S_HALF, yf, z, dev_p, land2.at[c, pl.ds(0, S_HALF)]),
            (S_HALF, ROWS, yf, z, dev_m, land2.at[c, pl.ds(S_HALF, ROWS - S_HALF)]),
            (S_LO, S_HI, yp, zb, dev_p, land2.at[c, pl.ds(ROWS, MIDDLE)]),
            (S_LO, S_HI, ym, zb, dev_m, land2.at[c, pl.ds(ROWS + MIDDLE, MIDDLE)]),
            (0, S_LO, yp, zb, dev_z, land2.at[c, pl.ds(EDGES, S_LO)]),
            (S_HI, ROWS, yp, zb, dev_z, land2.at[c, pl.ds(EDGES + S_LO, ROWS - S_HI)]),
            (0, S_LO, ym, zb, dev_z, land2.at[c, pl.ds(EDGES + EDGE, S_LO)]),
            (S_HI, ROWS, ym, zb, dev_z, land2.at[c, pl.ds(EDGES + EDGE + S_LO, ROWS - S_HI)]),
            (0, ROWS, yp, z, dev_p, land3.at[c, 0]),
            (0, ROWS, ym, z, dev_m, land3.at[c, 1]),
            (0, ROWS, y, zb, dev_z, land3.at[c, 2]),
        )[k - 15]
        return r_at(c, low, high, yy, zz), dst, dev

    def copy(c, k):
        src, dst, dev = gathered(c, k) if k < 15 else summed(c, k)
        return pltpu.make_async_remote_copy(
            src, dst, sent.at[k // 15], landed.at[c, GROUP_OF[k]], device_id=dev, device_id_type=MESH
        )

    def start(c, *ks):
        for k in ks:
            copy(c, k).start()

    def arrive(c, group):
        rows = land2.at[c, pl.ds(0, GROUP_ROWS[group])]
        pltpu.make_async_remote_copy(
            rows, rows, sent.at[0], landed.at[c, group], device_id=dev_z, device_id_type=MESH
        ).wait_recv()

    def gather_one(c):
        relay(c).wait_recv()
        start(c, 0, 1, 2)

    def gather_two(c):
        arrive(c, 1)
        start(c, 5, 7, 8)
        arrive(c, 2)
        start(c, 6, 9, 10)
        arrive(c, 0)
        start(c, 3, 4)

    def gather_three(c):
        arrive(c, 4)
        start(c, 11, 12)
        arrive(c, 3)
        start(c, 13, 14)

    def turn_weights(first, count):
        def body(i, carry):
            cols = pl.ds(pl.multiple_of((first + i) * TILE, TILE), TILE)
            turned = jnp.dot(wd[:, cols], hada[...], preferred_element_type=F32)
            wd[:, cols] = (turned * (1.0 / math.sqrt(128.0))).astype(BF16)
            return carry

        lax.fori_loop(0, count, body, 0)

    def compute(c):
        arrive(c, 5)

        def norm(i, carry):
            rows = pl.ds(pl.multiple_of(i * NORM_ROWS, NORM_ROWS), NORM_ROWS)
            wide = xg[c, rows, :].astype(F32)
            mean_square = jnp.sum(wide * wide, axis=1, keepdims=True) * (1.0 / D)
            nb[rows, :] = (wide * lax.rsqrt(mean_square + EPSILON) * gains[0:1, :]).astype(BF16)
            return carry

        lax.fori_loop(0, ROWS // NORM_ROWS, norm, 0)
        gate = jnp.dot(nb[...], wg[...], preferred_element_type=F32)
        up = jnp.dot(nb[...], wu[...], preferred_element_type=F32)
        hb[...] = (gate / (1.0 + jnp.exp(-gate)) * up).astype(BF16)
    def compute_out(c):
        term = jnp.dot(hb[...], wd[...], preferred_element_type=F32)
        for j in range(0, D, TILE):
            turned = term[:, j : j + TILE]
            squares = jnp.dot((turned * turned).astype(BF16), ones[...], preferred_element_type=F32)
            fourfold = squares * (CLIP_FACTOR**2 / 128.0) + CLIP_FACTOR**2 * BLOCK_EPSILON
            limit = fourfold * lax.rsqrt(fourfold)
            rot[c, :, j : j + TILE] = jnp.minimum(jnp.maximum(turned, -limit), limit).astype(BF16)
        start(c, 15, 16, 17, 18)

    def add(c, low, high, yy, zz, *others):
        total = rot[c, low:high, columns(yy, zz)].astype(F32)
        for other in others:
            total = total + other.astype(F32)
        rot[c, low:high, columns(yy, zz)] = total.astype(BF16)

    def sum_two(c):
        arrive(c, 6)
        add(c, 0, S_LO, yf, z, land1[c, 0:S_LO])
        add(c, S_HI, ROWS, yf, z, land1[c, S_HI:ROWS])
        start(c, 19, 20)
        arrive(c, 7)
        add(c, S_LO, S_HALF, yp, zb, land1[c, S_LO:S_HALF])
        start(c, 21)
        add(c, S_HALF, S_HI, ym, zb, land1[c, S_HALF:S_HI])
        start(c, 22, 23, 24, 25, 26)

    def sum_three(c):
        arrive(c, 8)
        add(c, 0, S_LO, yp, z, land2[c, 0:S_LO], land2[c, EDGES : EDGES + S_LO])
        add(c, S_LO, S_HALF, yp, z, land2[c, S_LO:S_HALF])
        add(c, S_HI, ROWS, yp, z, land2[c, EDGES + S_LO : EDGES + EDGE])
        start(c, 27)
        arrive(c, 9)
        add(c, 0, S_LO, ym, z, land2[c, EDGES + EDGE : EDGES + EDGE + S_LO])
        add(c, S_HALF, S_HI, ym, z, land2[c, S_HALF:S_HI])
        add(c, S_HI, ROWS, ym, z, land2[c, S_HI:ROWS], land2[c, EDGES + EDGE + S_LO : EDGES + 2 * EDGE])
        start(c, 28)
        arrive(c, 10)
        add(c, S_LO, S_HI, y, zb, land2[c, ROWS : ROWS + MIDDLE], land2[c, ROWS + MIDDLE : EDGES])
        start(c, 29)

    def finish(c):
        arrive(c, 11)
        out_rows = chunk_rows(c)
        for j in range(PART // 128):
            cols = pl.ds(pl.multiple_of((y * 2 + z) * PART + j * 128, 128), 128)
            here = slice(j * 128, (j + 1) * 128)
            total = rot[c, :, cols].astype(F32)
            for i in range(3):
                total = total + land3[c, i, :, here].astype(F32)
            high = total.astype(BF16)
            low = (total - high.astype(F32)).astype(BF16)
            table = hada[0:128, 0:128]
            update = jnp.dot(high, table, preferred_element_type=F32)
            update = update + jnp.dot(low, table, preferred_element_type=F32)
            incoming = xg[c, :, cols].astype(F32)
            out_ref[out_rows, here] = (incoming + update * (1.0 / math.sqrt(128.0))).astype(BF16)


    def step(i, carry):
        def stage(lag, work):
            @pl.when(jnp.logical_and(i >= lag, i < lag + CHUNKS))
            def _():
                work(i - lag)

        stage(0, gather_one)
        stage(1, gather_two)
        stage(2, gather_three)

        @pl.when(i == 0)
        def _():
            loads[0].wait()

        @pl.when(i < 3)
        def _():
            turn_weights(i * 4, 4)

        @pl.when(i == 3)
        def _():
            loads[1].wait()
            loads[2].wait()
            all_gains.wait_recv()

        stage(3, compute)
        stage(4, sum_two)
        stage(3, compute_out)
        stage(5, sum_three)
        stage(6, finish)
        return carry

    lax.fori_loop(0, CHUNKS + 6, step, 0)

    sevenths = xg.at[:, :, pl.ds(0, (N_TP - 1) * PART)]
    for phase in range(2):
        pltpu.make_async_remote_copy(
            sevenths, sevenths, sent.at[phase], gained, device_id=dev_z, device_id_type=MESH
        ).wait_send()

    @pl.when(has_next)
    def _():
        pltpu.make_async_remote_copy(
            prev_ref, prev_ref, sent.at[2], gained, device_id=next_dev, device_id_type=MESH
        ).wait_send()

    all_gains.wait_send()


def local(fresh_input, previous_out, norm_gain, gate_weight, up_weight, down_weight):
    anywhere = pl.BlockSpec(memory_space=pl.ANY)
    vmem = pl.BlockSpec(memory_space=pltpu.VMEM)
    dma = pltpu.SemaphoreType.DMA
    return pl.pallas_call(
        kernel,
        out_shape=pltpu.VMEM((TOK, PART), BF16),
        in_specs=[anywhere] * 6,
        out_specs=vmem,
        scratch_shapes=[
            pltpu.VMEM((CHUNKS, ROWS, D), BF16),
            pltpu.VMEM((D, H_DEV), BF16),
            pltpu.VMEM((D, H_DEV), BF16),
            pltpu.VMEM((H_DEV, D), BF16),
            pltpu.VMEM((CHUNKS, ROWS, D), BF16),
            pltpu.VMEM((CHUNKS, ROWS, PART), BF16),
            pltpu.VMEM((CHUNKS, 3 * ROWS, PART), BF16),
            pltpu.VMEM((CHUNKS, 3, ROWS, PART), BF16),
            pltpu.VMEM((ROWS, D), BF16),
            pltpu.VMEM((ROWS, H_DEV), BF16),
            pltpu.VMEM((8, D), F32),
            pltpu.VMEM((TILE, TILE), BF16),
            pltpu.VMEM((TILE, TILE), BF16),
            pltpu.VMEM((1, PART), BF16),
            dma(()),
            dma((3,)),
            dma((CHUNKS,)),
            dma(()),
            dma((4,)),
            dma((CHUNKS, len(GROUPS))),
        ],
        compiler_params=pltpu.CompilerParams(
            collective_id=0, has_side_effects=True, vmem_limit_bytes=56 << 20
        ),
        cost_estimate=pl.CostEstimate(
            flops=2 * 3 * TOK * D * H_DEV, bytes_accessed=3 * 2 * D * H_DEV, transcendentals=TOK * H_DEV
        ),
        name="relayed_feed_forward",
    )(fresh_input, previous_out, norm_gain, gate_weight, up_weight, down_weight)


def solution(mesh):
    in_specs = (
        P(None, "tp"),
        P("section", "tp"),
        P("section", "tp"),
        P("section", None, "tp"),
        P("section", None, "tp"),
        P("section", "tp", None),
    )
    return jax.shard_map(local, mesh=mesh, in_specs=in_specs, out_specs=P("section", "tp"), check_vma=False)
```

```python
import math

import jax
import jax.numpy as jnp
from jax import lax
from jax.experimental import pallas as pl
from jax.experimental.pallas import tpu as pltpu
from jax.sharding import PartitionSpec as P

EPSILON = 1e-05
BLOCK_EPSILON = 1e-06
CLIP_FACTOR = 2.0

MESH = pl.DeviceIdType.MESH
F32 = jnp.float32
BF16 = jnp.bfloat16

TOK = 1024
D = 3072
H_DEV = 1024
N_TP = 8
PART = 384
ROWS = 256
CHUNKS = TOK // ROWS
TILE = 256
NORM_ROWS = 64

LO, HALF, HI = 48, 128, 192
S_LO, S_HALF, S_HI = 64, 128, 208
MIDDLE = S_HI - S_LO
EDGE = ROWS - MIDDLE
EDGES = ROWS + 2 * MIDDLE

GROUPS = (
    (0,), (1,), (2,), (3, 4), (5, 6), (7, 8, 9, 10, 11, 12, 13, 14),
    (15, 16), (17, 18), (19, 23, 24), (20, 25, 26), (21, 22), (27, 28, 29),
)
GROUP_OF = {k: group for group, ks in enumerate(GROUPS) for k in ks}
GROUP_ROWS = (
    ROWS, ROWS, ROWS, 2 * (HI - LO), ROWS, 3 * (ROWS - HI + LO) + HI - LO,
    EDGE, MIDDLE, S_HALF + EDGE, ROWS - S_HALF + EDGE, 2 * MIDDLE, 3 * ROWS,
)


def kernel(
    fresh_ref, prev_ref, gain_ref, gate_ref, up_ref, down_ref, out_ref,
    xg, wg, wu, wd, rot, land1, land2, land3, nb, hb, gains, hada, ones, gain,
    gain_sem, load_sem, relayed, gained, sent, landed,
):
    s = lax.axis_index("section")
    t = lax.axis_index("tp")
    n_sections = lax.axis_size("section")
    n_tp = lax.axis_size("tp")
    y, z = t // 2, t % 2
    core = s % 2
    yp, ym, yf = (y + 1) % 4, (y + 3) % 4, (y + 2) % 4
    zb = 1 - z
    dev_p, dev_m, dev_z = (s, yp * 2 + z), (s, ym * 2 + z), (s, y * 2 + zb)
    has_next = s < n_sections - 1
    has_prev = s > 0
    next_dev = (jnp.minimum(s + 1, n_sections - 1), jnp.where(core == 0, t, y * 2 + zb))
    prev_dev = (jnp.maximum(s - 1, 0), jnp.where(core == 1, t, y * 2 + zb))
    zo = jnp.where(jnp.logical_or(core == 1, s == 0), z, zb)
    zq = 1 - zo

    loads = [
        pltpu.make_async_copy(src, dst, load_sem.at[i])
        for i, (src, dst) in enumerate(((down_ref.at[0], wd), (gate_ref.at[0], wg), (up_ref.at[0], wu)))
    ]
    barrier = pltpu.get_barrier_semaphore()
    for q in range(1, n_tp):
        pl.semaphore_signal(barrier, inc=1, device_id=(s, (t + q) % n_tp), device_id_type=MESH)

    around = (t, y * 2 + zb, yp * 2 + z, ym * 2 + z)

    @pl.when(core == 0)
    def _():
        for at in around:
            pl.semaphore_signal(barrier, inc=1, device_id=(s + 1, at), device_id_type=MESH)

    @pl.when(core == 1)
    def _():
        for at in around:
            pl.semaphore_signal(barrier, inc=1, device_id=(s - 1, at), device_id_type=MESH)

    far_next = jnp.logical_and(core == 1, has_next)
    far_prev = jnp.logical_and(core == 0, has_prev)

    @pl.when(far_next)
    def _():
        pl.semaphore_signal(barrier, inc=1, device_id=next_dev, device_id_type=MESH)

    @pl.when(far_prev)
    def _():
        pl.semaphore_signal(barrier, inc=1, device_id=prev_dev, device_id_type=MESH)

    gain_load = pltpu.make_async_copy(gain_ref, gain, gain_sem)
    gain_load.start()
    for load in loads:
        load.start()

    pl.semaphore_wait(barrier, n_tp + 3 + far_next.astype(jnp.int32) + far_prev.astype(jnp.int32))

    def columns(yy, zz):
        return pl.ds(pl.multiple_of((yy * 2 + zz) * PART, 128), PART)

    def chunk_rows(c):
        return pl.ds(pl.multiple_of(c * ROWS, ROWS), ROWS)

    def relay(c):
        return pltpu.make_async_remote_copy(
            prev_ref.at[chunk_rows(c)],
            xg.at[c, :, columns(y, z)],
            sent.at[2],
            relayed.at[c],
            device_id=next_dev,
            device_id_type=MESH,
        )

    @pl.when(core == 0)
    def _():
        for d in range(3):
            pltpu.make_async_remote_copy(
                prev_ref.at[pl.ds(0, ROWS)],
                xg.at[0, :, columns(y, z)],
                sent.at[2],
                landed.at[0, d],
                device_id=(s + 1, around[d + 1]),
                device_id_type=MESH,
            ).start()

    @pl.when(has_next)
    def _():
        for c in range(CHUNKS):
            relay(c).start()

    @pl.when(s == 0)
    def _():
        for c in range(CHUNKS):
            pltpu.make_async_copy(
                fresh_ref.at[chunk_rows(c)], xg.at[c, :, columns(y, z)], relayed.at[c]
            ).start()

    def gain_copy(cols, dev):
        row = gains.at[pl.ds(0, 1), cols]
        return pltpu.make_async_remote_copy(
            row, row, sent.at[3], gained, device_id=dev, device_id_type=MESH
        )

    all_gains = gain_copy(pl.ds(0, (N_TP - 1) * PART), dev_z)

    row_id = lax.broadcasted_iota(jnp.int32, (TILE, TILE), 0)
    col_id = lax.broadcasted_iota(jnp.int32, (TILE, TILE), 1)
    common = (row_id & col_id) & 127
    parity = common
    for shift in (4, 2, 1):
        parity = parity ^ (parity >> shift)
    same = (row_id >> 7) == (col_id >> 7)
    hada[...] = jnp.where(same, (1 - 2 * (parity & 1)).astype(F32), 0.0).astype(BF16)
    ones[...] = jnp.where(same, 1.0, 0.0).astype(BF16)

    def x_at(c, low, high, yy, zz):
        return xg.at[c, pl.ds(low, high - low), columns(yy, zz)]

    def r_at(c, low, high, yy, zz):
        return rot.at[c, pl.ds(low, high - low), columns(yy, zz)]

    def gathered(c, k):
        low, high, yy, zz, dev = (
            (0, ROWS, y, zo, dev_z),
            (0, ROWS, y, zo, dev_p),
            (0, ROWS, y, zo, dev_m),
            (LO, HI, y, zq, dev_p),
            (LO, HI, y, zq, dev_m),
            (0, HALF, ym, zo, dev_p),
            (HALF, ROWS, yp, zo, dev_m),
            (0, LO, ym, zo, dev_z),
            (HI, ROWS, ym, zo, dev_z),
            (0, LO, yp, zo, dev_z),
            (HI, ROWS, yp, zo, dev_z),
            (0, LO, yf, zo, dev_z),
            (HI, ROWS, yf, zo, dev_z),
            (LO, HALF, ym, zq, dev_p),
            (HALF, HI, yp, zq, dev_m),
        )[k]
        ref = x_at(c, low, high, yy, zz)
        return ref, ref, dev

    def summed(c, k):
        low, high, yy, zz, dev, dst = (
            (0, S_LO, yf, zb, dev_z, land1.at[c, pl.ds(0, S_LO)]),
            (S_HI, ROWS, yf, zb, dev_z, land1.at[c, pl.ds(S_HI, ROWS - S_HI)]),
            (S_LO, S_HALF, yf, zb, dev_p, land1.at[c, pl.ds(S_LO, S_HALF - S_LO)]),
            (S_HALF, S_HI, yf, zb, dev_m, land1.at[c, pl.ds(S_HALF, S_HI - S_HALF)]),
            (0, S_HALF, yf, z, dev_p, land2.at[c, pl.ds(0, S_HALF)]),
            (S_HALF, ROWS, yf, z, dev_m, land2.at[c, pl.ds(S_HALF, ROWS - S_HALF)]),
            (S_LO, S_HI, yp, zb, dev_p, land2.at[c, pl.ds(ROWS, MIDDLE)]),
            (S_LO, S_HI, ym, zb, dev_m, land2.at[c, pl.ds(ROWS + MIDDLE, MIDDLE)]),
            (0, S_LO, yp, zb, dev_z, land2.at[c, pl.ds(EDGES, S_LO)]),
            (S_HI, ROWS, yp, zb, dev_z, land2.at[c, pl.ds(EDGES + S_LO, ROWS - S_HI)]),
            (0, S_LO, ym, zb, dev_z, land2.at[c, pl.ds(EDGES + EDGE, S_LO)]),
            (S_HI, ROWS, ym, zb, dev_z, land2.at[c, pl.ds(EDGES + EDGE + S_LO, ROWS - S_HI)]),
            (0, ROWS, yp, z, dev_p, land3.at[c, 0]),
            (0, ROWS, ym, z, dev_m, land3.at[c, 1]),
            (0, ROWS, y, zb, dev_z, land3.at[c, 2]),
        )[k - 15]
        return r_at(c, low, high, yy, zz), dst, dev

    def copy(c, k):
        src, dst, dev = gathered(c, k) if k < 15 else summed(c, k)
        return pltpu.make_async_remote_copy(
            src, dst, sent.at[4 if k < 3 else k // 15], landed.at[c, GROUP_OF[k]], device_id=dev, device_id_type=MESH
        )

    def start(c, *ks):
        for k in ks:
            copy(c, k).start()

    def arrive(c, group):
        rows = land2.at[c, pl.ds(0, GROUP_ROWS[group])]
        pltpu.make_async_remote_copy(
            rows, rows, sent.at[0], landed.at[c, group], device_id=dev_z, device_id_type=MESH
        ).wait_recv()

    def gather_one(c):
        relay(c).wait_recv()

        @pl.when(jnp.logical_or(c > 0, core == 0))
        def _():
            start(c, 0, 1, 2)

    def gather_two(c):
        arrive(c, 1)
        start(c, 5, 7, 8)
        arrive(c, 2)
        start(c, 6, 9, 10)
        arrive(c, 0)
        start(c, 3, 4)

    def gather_three(c):
        arrive(c, 4)
        start(c, 11, 12)
        arrive(c, 3)
        start(c, 13, 14)

    def turn_weights(first, count):
        def body(i, carry):
            cols = pl.ds(pl.multiple_of((first + i) * TILE, TILE), TILE)
            turned = jnp.dot(wd[:, cols], hada[...], preferred_element_type=F32)
            wd[:, cols] = (turned * (1.0 / math.sqrt(128.0))).astype(BF16)
            return carry

        lax.fori_loop(0, count, body, 0)

    def compute(c):
        arrive(c, 5)

        def norm(i, carry):
            rows = pl.ds(pl.multiple_of(i * NORM_ROWS, NORM_ROWS), NORM_ROWS)
            wide = xg[c, rows, :].astype(F32)
            mean_square = jnp.sum(wide * wide, axis=1, keepdims=True) * (1.0 / D)
            nb[rows, :] = (wide * lax.rsqrt(mean_square + EPSILON) * gains[0:1, :]).astype(BF16)
            return carry

        lax.fori_loop(0, ROWS // NORM_ROWS, norm, 0)
        gate = jnp.dot(nb[...], wg[...], preferred_element_type=F32)
        up = jnp.dot(nb[...], wu[...], preferred_element_type=F32)
        hb[...] = (gate / (1.0 + jnp.exp(-gate)) * up).astype(BF16)
    def compute_out(c):
        term = jnp.dot(hb[...], wd[...], preferred_element_type=F32)
        for j in range(0, D, TILE):
            turned = term[:, j : j + TILE]
            squares = jnp.dot((turned * turned).astype(BF16), ones[...], preferred_element_type=F32)
            fourfold = squares * (CLIP_FACTOR**2 / 128.0) + CLIP_FACTOR**2 * BLOCK_EPSILON
            limit = fourfold * lax.rsqrt(fourfold)
            rot[c, :, j : j + TILE] = jnp.minimum(jnp.maximum(turned, -limit), limit).astype(BF16)
        start(c, 15, 16, 17, 18)

    def add(c, low, high, yy, zz, *others):
        total = rot[c, low:high, columns(yy, zz)].astype(F32)
        for other in others:
            total = total + other.astype(F32)
        rot[c, low:high, columns(yy, zz)] = total.astype(BF16)

    def sum_two(c):
        arrive(c, 6)
        add(c, 0, S_LO, yf, z, land1[c, 0:S_LO])
        add(c, S_HI, ROWS, yf, z, land1[c, S_HI:ROWS])
        start(c, 19, 20)
        arrive(c, 7)
        add(c, S_LO, S_HALF, yp, zb, land1[c, S_LO:S_HALF])
        start(c, 21)
        add(c, S_HALF, S_HI, ym, zb, land1[c, S_HALF:S_HI])
        start(c, 22, 23, 24, 25, 26)

    def sum_three(c):
        arrive(c, 8)
        add(c, 0, S_LO, yp, z, land2[c, 0:S_LO], land2[c, EDGES : EDGES + S_LO])
        add(c, S_LO, S_HALF, yp, z, land2[c, S_LO:S_HALF])
        add(c, S_HI, ROWS, yp, z, land2[c, EDGES + S_LO : EDGES + EDGE])
        start(c, 27)
        arrive(c, 9)
        add(c, 0, S_LO, ym, z, land2[c, EDGES + EDGE : EDGES + EDGE + S_LO])
        add(c, S_HALF, S_HI, ym, z, land2[c, S_HALF:S_HI])
        add(c, S_HI, ROWS, ym, z, land2[c, S_HI:ROWS], land2[c, EDGES + EDGE + S_LO : EDGES + 2 * EDGE])
        start(c, 28)
        arrive(c, 10)
        add(c, S_LO, S_HI, y, zb, land2[c, ROWS : ROWS + MIDDLE], land2[c, ROWS + MIDDLE : EDGES])
        start(c, 29)

    def finish(c):
        arrive(c, 11)
        out_rows = chunk_rows(c)
        for j in range(PART // 128):
            cols = pl.ds(pl.multiple_of((y * 2 + z) * PART + j * 128, 128), 128)
            here = slice(j * 128, (j + 1) * 128)
            total = rot[c, :, cols].astype(F32)
            for i in range(3):
                total = total + land3[c, i, :, here].astype(F32)
            high = total.astype(BF16)
            low = (total - high.astype(F32)).astype(BF16)
            table = hada[0:128, 0:128]
            update = jnp.dot(high, table, preferred_element_type=F32)
            update = update + jnp.dot(low, table, preferred_element_type=F32)
            incoming = xg[c, :, cols].astype(F32)
            out_ref[out_rows, here] = (incoming + update * (1.0 / math.sqrt(128.0))).astype(BF16)


    def step(i, carry):
        def stage(lag, work):
            @pl.when(jnp.logical_and(i >= lag, i < lag + CHUNKS))
            def _():
                work(i - lag)

        stage(0, gather_one)

        @pl.when(i == 0)
        def _():
            gain_load.wait()
            gains[0:1, columns(y, z)] = gain[...].astype(F32)
            for q in range(1, n_tp):
                gain_copy(columns(y, z), (s, (t + q) % n_tp)).start()

        stage(1, gather_two)
        stage(2, gather_three)

        @pl.when(i == 0)
        def _():
            loads[0].wait()

        @pl.when(i < 3)
        def _():
            turn_weights(i * 4, 4)

        @pl.when(i == 3)
        def _():
            loads[1].wait()
            loads[2].wait()
            all_gains.wait_recv()

        stage(3, compute)
        stage(4, sum_two)
        stage(3, compute_out)
        stage(5, sum_three)
        stage(6, finish)
        return carry

    lax.fori_loop(0, CHUNKS + 6, step, 0)

    def all_sent(ref, sem):
        pltpu.make_async_remote_copy(
            ref, ref, sent.at[sem], gained, device_id=dev_z, device_id_type=MESH
        ).wait_send()

    all_sent(xg.at[:, :, pl.ds(0, 4 * PART)], 0)
    all_sent(xg.at[:, :, pl.ds(0, 7 * PART)], 1)

    @pl.when(core == 0)
    def _():
        all_sent(xg.at[:, :, pl.ds(0, 3 * PART)], 4)
        all_sent(xg.at[0, :, pl.ds(0, (CHUNKS + 3) * PART)], 2)

    @pl.when(core == 1)
    def _():
        all_sent(xg.at[pl.ds(0, CHUNKS - 1), :, pl.ds(0, 3 * PART)], 4)

    @pl.when(far_next)
    def _():
        all_sent(xg.at[0, :, pl.ds(0, CHUNKS * PART)], 2)

    all_gains.wait_send()


def local(fresh_input, previous_out, norm_gain, gate_weight, up_weight, down_weight):
    anywhere = pl.BlockSpec(memory_space=pl.ANY)
    vmem = pl.BlockSpec(memory_space=pltpu.VMEM)
    dma = pltpu.SemaphoreType.DMA
    return pl.pallas_call(
        kernel,
        out_shape=pltpu.VMEM((TOK, PART), BF16),
        in_specs=[anywhere] * 6,
        out_specs=vmem,
        scratch_shapes=[
            pltpu.VMEM((CHUNKS, ROWS, D), BF16),
            pltpu.VMEM((D, H_DEV), BF16),
            pltpu.VMEM((D, H_DEV), BF16),
            pltpu.VMEM((H_DEV, D), BF16),
            pltpu.VMEM((CHUNKS, ROWS, D), BF16),
            pltpu.VMEM((CHUNKS, ROWS, PART), BF16),
            pltpu.VMEM((CHUNKS, 3 * ROWS, PART), BF16),
            pltpu.VMEM((CHUNKS, 3, ROWS, PART), BF16),
            pltpu.VMEM((ROWS, D), BF16),
            pltpu.VMEM((ROWS, H_DEV), BF16),
            pltpu.VMEM((8, D), F32),
            pltpu.VMEM((TILE, TILE), BF16),
            pltpu.VMEM((TILE, TILE), BF16),
            pltpu.VMEM((1, PART), BF16),
            dma(()),
            dma((3,)),
            dma((CHUNKS,)),
            dma(()),
            dma((5,)),
            dma((CHUNKS, len(GROUPS))),
        ],
        compiler_params=pltpu.CompilerParams(
            collective_id=0, has_side_effects=True, vmem_limit_bytes=56 << 20
        ),
        cost_estimate=pl.CostEstimate(
            flops=2 * 3 * TOK * D * H_DEV, bytes_accessed=3 * 2 * D * H_DEV, transcendentals=TOK * H_DEV
        ),
        name="relayed_feed_forward",
    )(fresh_input, previous_out, norm_gain, gate_weight, up_weight, down_weight)


def solution(mesh):
    in_specs = (
        P(None, "tp"),
        P("section", "tp"),
        P("section", "tp"),
        P("section", None, "tp"),
        P("section", None, "tp"),
        P("section", "tp", None),
    )
    return jax.shard_map(local, mesh=mesh, in_specs=in_specs, out_specs=P("section", "tp"), check_vma=False)
```

```python
import math

import jax
import jax.numpy as jnp
from jax import lax
from jax.experimental import pallas as pl
from jax.experimental.pallas import tpu as pltpu
from jax.sharding import PartitionSpec as P

EPSILON = 1e-05
BLOCK_EPSILON = 1e-06
CLIP_FACTOR = 2.0

MESH = pl.DeviceIdType.MESH
F32 = jnp.float32
BF16 = jnp.bfloat16

TOK = 1024
D = 3072
H_DEV = 1024
N_TP = 8
PART = 384
ROWS = 256
CHUNKS = TOK // ROWS
TILE = 256
NORM_ROWS = 64

LO, HALF, HI = 48, 128, 192
S_LO, S_HALF, S_HI = 64, 128, 208
MIDDLE = S_HI - S_LO
EDGE = ROWS - MIDDLE
EDGES = ROWS + 2 * MIDDLE

GROUPS = (
    (0,), (1,), (2,), (3, 4), (5, 6), (7, 8, 9, 10, 11, 12, 13, 14),
    (15, 16), (17, 18), (19, 23, 24), (20, 25, 26), (21, 22), (27, 28, 29),
)
GROUP_OF = {k: group for group, ks in enumerate(GROUPS) for k in ks}
GROUP_ROWS = (
    ROWS, ROWS, ROWS, 2 * (HI - LO), ROWS, 3 * (ROWS - HI + LO) + HI - LO,
    EDGE, MIDDLE, S_HALF + EDGE, ROWS - S_HALF + EDGE, 2 * MIDDLE, 3 * ROWS,
)


def kernel(
    fresh_ref, prev_ref, gain_ref, gate_ref, up_ref, down_ref, out_ref,
    xg, wg, wu, wd, rot, land1, land2, land3, nb, hb, gains, hada, ones, gain,
    gain_sem, load_sem, relayed, gained, sent, landed,
):
    s = lax.axis_index("section")
    t = lax.axis_index("tp")
    n_sections = lax.axis_size("section")
    n_tp = lax.axis_size("tp")
    y, z = t // 2, t % 2
    core = s % 2
    yp, ym, yf = (y + 1) % 4, (y + 3) % 4, (y + 2) % 4
    zb = 1 - z
    dev_p, dev_m, dev_z = (s, yp * 2 + z), (s, ym * 2 + z), (s, y * 2 + zb)
    has_next = s < n_sections - 1
    has_prev = s > 0
    next_dev = (jnp.minimum(s + 1, n_sections - 1), jnp.where(core == 0, t, y * 2 + zb))
    prev_dev = (jnp.maximum(s - 1, 0), jnp.where(core == 1, t, y * 2 + zb))
    zo = jnp.where(jnp.logical_or(core == 1, s == 0), z, zb)
    zq = 1 - zo

    loads = [
        pltpu.make_async_copy(src, dst, load_sem.at[i])
        for i, (src, dst) in enumerate(((down_ref.at[0], wd), (gate_ref.at[0], wg), (up_ref.at[0], wu)))
    ]
    barrier = pltpu.get_barrier_semaphore()
    for q in range(1, n_tp):
        pl.semaphore_signal(barrier, inc=1, device_id=(s, (t + q) % n_tp), device_id_type=MESH)

    around = (t, y * 2 + zb, yp * 2 + z, ym * 2 + z)

    @pl.when(core == 0)
    def _():
        for at in around:
            pl.semaphore_signal(barrier, inc=1, device_id=(s + 1, at), device_id_type=MESH)

    @pl.when(core == 1)
    def _():
        for at in around:
            pl.semaphore_signal(barrier, inc=1, device_id=(s - 1, at), device_id_type=MESH)

    far_next = jnp.logical_and(core == 1, has_next)
    far_prev = jnp.logical_and(core == 0, has_prev)

    @pl.when(far_next)
    def _():
        pl.semaphore_signal(barrier, inc=1, device_id=next_dev, device_id_type=MESH)

    @pl.when(far_prev)
    def _():
        pl.semaphore_signal(barrier, inc=1, device_id=prev_dev, device_id_type=MESH)

    gain_load = pltpu.make_async_copy(gain_ref, gain, gain_sem)
    gain_load.start()
    for load in loads:
        load.start()

    pl.semaphore_wait(barrier, n_tp + 3 + far_next.astype(jnp.int32) + far_prev.astype(jnp.int32))

    def columns(yy, zz):
        return pl.ds(pl.multiple_of((yy * 2 + zz) * PART, 128), PART)

    def chunk_rows(c):
        return pl.ds(pl.multiple_of(c * ROWS, ROWS), ROWS)

    def relay(c):
        return pltpu.make_async_remote_copy(
            prev_ref.at[chunk_rows(c)],
            xg.at[c, :, columns(y, z)],
            sent.at[2],
            relayed.at[c],
            device_id=next_dev,
            device_id_type=MESH,
        )

    @pl.when(core == 0)
    def _():
        for d in range(3):
            pltpu.make_async_remote_copy(
                prev_ref.at[pl.ds(0, ROWS)],
                xg.at[0, :, columns(y, z)],
                sent.at[2],
                landed.at[0, d],
                device_id=(s + 1, around[d + 1]),
                device_id_type=MESH,
            ).start()

    @pl.when(has_next)
    def _():
        for c in range(CHUNKS):
            relay(c).start()

    @pl.when(s == 0)
    def _():
        for c in range(CHUNKS):
            pltpu.make_async_copy(
                fresh_ref.at[chunk_rows(c)], xg.at[c, :, columns(y, z)], relayed.at[c]
            ).start()

    def gain_copy(cols, dev):
        row = gains.at[pl.ds(0, 1), cols]
        return pltpu.make_async_remote_copy(
            row, row, sent.at[3], gained, device_id=dev, device_id_type=MESH
        )

    all_gains = gain_copy(pl.ds(0, (N_TP - 1) * PART), dev_z)

    row_id = lax.broadcasted_iota(jnp.int32, (TILE, TILE), 0)
    col_id = lax.broadcasted_iota(jnp.int32, (TILE, TILE), 1)
    common = (row_id & col_id) & 127
    parity = common
    for shift in (4, 2, 1):
        parity = parity ^ (parity >> shift)
    same = (row_id >> 7) == (col_id >> 7)
    hada[...] = jnp.where(same, (1 - 2 * (parity & 1)).astype(F32), 0.0).astype(BF16)
    ones[...] = jnp.where(same, 1.0, 0.0).astype(BF16)

    def x_at(c, low, high, yy, zz):
        return xg.at[c, pl.ds(low, high - low), columns(yy, zz)]

    def r_at(c, low, high, yy, zz):
        return rot.at[c, pl.ds(low, high - low), columns(yy, zz)]

    def gathered(c, k):
        low, high, yy, zz, dev = (
            (0, ROWS, y, zo, dev_z),
            (0, ROWS, y, zo, dev_p),
            (0, ROWS, y, zo, dev_m),
            (LO, HI, y, zq, dev_p),
            (LO, HI, y, zq, dev_m),
            (0, HALF, ym, zo, dev_p),
            (HALF, ROWS, yp, zo, dev_m),
            (0, LO, ym, zo, dev_z),
            (HI, ROWS, ym, zo, dev_z),
            (0, LO, yp, zo, dev_z),
            (HI, ROWS, yp, zo, dev_z),
            (0, LO, yf, zo, dev_z),
            (HI, ROWS, yf, zo, dev_z),
            (LO, HALF, ym, zq, dev_p),
            (HALF, HI, yp, zq, dev_m),
        )[k]
        ref = x_at(c, low, high, yy, zz)
        return ref, ref, dev

    def summed(c, k):
        low, high, yy, zz, dev, dst = (
            (0, S_LO, yf, zb, dev_z, land1.at[c, pl.ds(0, S_LO)]),
            (S_HI, ROWS, yf, zb, dev_z, land1.at[c, pl.ds(S_HI, ROWS - S_HI)]),
            (S_LO, S_HALF, yf, zb, dev_p, land1.at[c, pl.ds(S_LO, S_HALF - S_LO)]),
            (S_HALF, S_HI, yf, zb, dev_m, land1.at[c, pl.ds(S_HALF, S_HI - S_HALF)]),
            (0, S_HALF, yf, z, dev_p, land2.at[c, pl.ds(0, S_HALF)]),
            (S_HALF, ROWS, yf, z, dev_m, land2.at[c, pl.ds(S_HALF, ROWS - S_HALF)]),
            (S_LO, S_HI, yp, zb, dev_p, land2.at[c, pl.ds(ROWS, MIDDLE)]),
            (S_LO, S_HI, ym, zb, dev_m, land2.at[c, pl.ds(ROWS + MIDDLE, MIDDLE)]),
            (0, S_LO, yp, zb, dev_z, land2.at[c, pl.ds(EDGES, S_LO)]),
            (S_HI, ROWS, yp, zb, dev_z, land2.at[c, pl.ds(EDGES + S_LO, ROWS - S_HI)]),
            (0, S_LO, ym, zb, dev_z, land2.at[c, pl.ds(EDGES + EDGE, S_LO)]),
            (S_HI, ROWS, ym, zb, dev_z, land2.at[c, pl.ds(EDGES + EDGE + S_LO, ROWS - S_HI)]),
            (0, ROWS, yp, z, dev_p, land3.at[c, 0]),
            (0, ROWS, ym, z, dev_m, land3.at[c, 1]),
            (0, ROWS, y, zb, dev_z, land3.at[c, 2]),
        )[k - 15]
        return r_at(c, low, high, yy, zz), dst, dev

    def copy(c, k):
        src, dst, dev = gathered(c, k) if k < 15 else summed(c, k)
        return pltpu.make_async_remote_copy(
            src, dst, sent.at[4 if k < 3 else k // 15], landed.at[c, GROUP_OF[k]], device_id=dev, device_id_type=MESH
        )

    def start(c, *ks):
        for k in ks:
            copy(c, k).start()

    def arrive(c, group):
        rows = land2.at[c, pl.ds(0, GROUP_ROWS[group])]
        pltpu.make_async_remote_copy(
            rows, rows, sent.at[0], landed.at[c, group], device_id=dev_z, device_id_type=MESH
        ).wait_recv()

    def gather_one(c):
        relay(c).wait_recv()

        @pl.when(jnp.logical_or(c > 0, core == 0))
        def _():
            start(c, 0, 1, 2)

    def gather_two(c):
        arrive(c, 1)
        start(c, 5, 7, 8)
        arrive(c, 2)
        start(c, 6, 9, 10)
        arrive(c, 0)
        start(c, 3, 4)

    def gather_three(c):
        arrive(c, 4)
        start(c, 11, 12)
        arrive(c, 3)
        start(c, 13, 14)

    def turn_weights(first, count):
        def body(i, carry):
            cols = pl.ds(pl.multiple_of((first + i) * TILE, TILE), TILE)
            turned = jnp.dot(wd[:, cols], hada[...], preferred_element_type=F32)
            wd[:, cols] = (turned * (1.0 / math.sqrt(128.0))).astype(BF16)
            return carry

        lax.fori_loop(0, count, body, 0)

    def compute(c):
        arrive(c, 5)

        def norm(i, carry):
            rows = pl.ds(pl.multiple_of(i * NORM_ROWS, NORM_ROWS), NORM_ROWS)
            wide = xg[c, rows, :].astype(F32)
            mean_square = jnp.sum(wide * wide, axis=1, keepdims=True) * (1.0 / D)
            nb[rows, :] = (wide * lax.rsqrt(mean_square + EPSILON) * gains[0:1, :]).astype(BF16)
            return carry

        lax.fori_loop(0, ROWS // NORM_ROWS, norm, 0)
        gate = jnp.dot(nb[...], wg[...], preferred_element_type=F32)
        up = jnp.dot(nb[...], wu[...], preferred_element_type=F32)
        hb[...] = (gate / (1.0 + jnp.exp(-gate)) * up).astype(BF16)
    def compute_out(c):
        term = jnp.dot(hb[...], wd[...], preferred_element_type=F32)
        for j in range(0, D, TILE):
            turned = term[:, j : j + TILE]
            squares = jnp.dot((turned * turned).astype(BF16), ones[...], preferred_element_type=F32)
            fourfold = squares * (CLIP_FACTOR**2 / 128.0) + CLIP_FACTOR**2 * BLOCK_EPSILON
            limit = fourfold * lax.rsqrt(fourfold)
            rot[c, :, j : j + TILE] = jnp.minimum(jnp.maximum(turned, -limit), limit).astype(BF16)
        start(c, 15, 16, 17, 18)

        @pl.when(c == CHUNKS - 1)
        def _():
            start(c, 23, 24, 25, 26)

    def add(c, low, high, yy, zz, *others):
        total = rot[c, low:high, columns(yy, zz)].astype(F32)
        for other in others:
            total = total + other.astype(F32)
        rot[c, low:high, columns(yy, zz)] = total.astype(BF16)

    def sum_two(c):
        arrive(c, 6)
        add(c, 0, S_LO, yf, z, land1[c, 0:S_LO])
        add(c, S_HI, ROWS, yf, z, land1[c, S_HI:ROWS])
        start(c, 19, 20)
        arrive(c, 7)
        add(c, S_LO, S_HALF, yp, zb, land1[c, S_LO:S_HALF])
        start(c, 21)
        add(c, S_HALF, S_HI, ym, zb, land1[c, S_HALF:S_HI])
        start(c, 22)

        @pl.when(c < CHUNKS - 1)
        def _():
            start(c, 23, 24, 25, 26)

    def sum_three(c):
        arrive(c, 8)
        add(c, 0, S_LO, yp, z, land2[c, 0:S_LO], land2[c, EDGES : EDGES + S_LO])
        add(c, S_LO, S_HALF, yp, z, land2[c, S_LO:S_HALF])
        add(c, S_HI, ROWS, yp, z, land2[c, EDGES + S_LO : EDGES + EDGE])
        start(c, 27)
        arrive(c, 9)
        add(c, 0, S_LO, ym, z, land2[c, EDGES + EDGE : EDGES + EDGE + S_LO])
        add(c, S_HALF, S_HI, ym, z, land2[c, S_HALF:S_HI])
        add(c, S_HI, ROWS, ym, z, land2[c, S_HI:ROWS], land2[c, EDGES + EDGE + S_LO : EDGES + 2 * EDGE])
        start(c, 28)
        arrive(c, 10)
        add(c, S_LO, S_HI, y, zb, land2[c, ROWS : ROWS + MIDDLE], land2[c, ROWS + MIDDLE : EDGES])
        start(c, 29)

    def finish(c):
        arrive(c, 11)
        out_rows = chunk_rows(c)
        for j in range(PART // 128):
            cols = pl.ds(pl.multiple_of((y * 2 + z) * PART + j * 128, 128), 128)
            here = slice(j * 128, (j + 1) * 128)
            total = rot[c, :, cols].astype(F32)
            for i in range(3):
                total = total + land3[c, i, :, here].astype(F32)
            high = total.astype(BF16)
            low = (total - high.astype(F32)).astype(BF16)
            table = hada[0:128, 0:128]
            update = jnp.dot(high, table, preferred_element_type=F32)
            update = update + jnp.dot(low, table, preferred_element_type=F32)
            incoming = xg[c, :, cols].astype(F32)
            out_ref[out_rows, here] = (incoming + update * (1.0 / math.sqrt(128.0))).astype(BF16)


    def step(i, carry):
        def stage(lag, work):
            @pl.when(jnp.logical_and(i >= lag, i < lag + CHUNKS))
            def _():
                work(i - lag)

        stage(0, gather_one)

        @pl.when(i == 0)
        def _():
            gain_load.wait()
            gains[0:1, columns(y, z)] = gain[...].astype(F32)
            for q in range(1, n_tp):
                gain_copy(columns(y, z), (s, (t + q) % n_tp)).start()

        stage(1, gather_two)
        stage(2, gather_three)

        @pl.when(i == 0)
        def _():
            loads[0].wait()

        @pl.when(i < 3)
        def _():
            turn_weights(i * 4, 4)

        @pl.when(i == 3)
        def _():
            loads[1].wait()
            loads[2].wait()
            all_gains.wait_recv()

        stage(3, compute)
        stage(4, sum_two)
        stage(3, compute_out)
        stage(5, sum_three)
        stage(6, finish)
        return carry

    lax.fori_loop(0, CHUNKS + 6, step, 0)

    def all_sent(ref, sem):
        pltpu.make_async_remote_copy(
            ref, ref, sent.at[sem], gained, device_id=dev_z, device_id_type=MESH
        ).wait_send()

    all_sent(xg.at[:, :, pl.ds(0, 4 * PART)], 0)
    all_sent(xg.at[:, :, pl.ds(0, 7 * PART)], 1)

    @pl.when(core == 0)
    def _():
        all_sent(xg.at[:, :, pl.ds(0, 3 * PART)], 4)
        all_sent(xg.at[0, :, pl.ds(0, (CHUNKS + 3) * PART)], 2)

    @pl.when(core == 1)
    def _():
        all_sent(xg.at[pl.ds(0, CHUNKS - 1), :, pl.ds(0, 3 * PART)], 4)

    @pl.when(far_next)
    def _():
        all_sent(xg.at[0, :, pl.ds(0, CHUNKS * PART)], 2)

    all_gains.wait_send()


def local(fresh_input, previous_out, norm_gain, gate_weight, up_weight, down_weight):
    anywhere = pl.BlockSpec(memory_space=pl.ANY)
    vmem = pl.BlockSpec(memory_space=pltpu.VMEM)
    dma = pltpu.SemaphoreType.DMA
    return pl.pallas_call(
        kernel,
        out_shape=pltpu.VMEM((TOK, PART), BF16),
        in_specs=[anywhere] * 6,
        out_specs=vmem,
        scratch_shapes=[
            pltpu.VMEM((CHUNKS, ROWS, D), BF16),
            pltpu.VMEM((D, H_DEV), BF16),
            pltpu.VMEM((D, H_DEV), BF16),
            pltpu.VMEM((H_DEV, D), BF16),
            pltpu.VMEM((CHUNKS, ROWS, D), BF16),
            pltpu.VMEM((CHUNKS, ROWS, PART), BF16),
            pltpu.VMEM((CHUNKS, 3 * ROWS, PART), BF16),
            pltpu.VMEM((CHUNKS, 3, ROWS, PART), BF16),
            pltpu.VMEM((ROWS, D), BF16),
            pltpu.VMEM((ROWS, H_DEV), BF16),
            pltpu.VMEM((8, D), F32),
            pltpu.VMEM((TILE, TILE), BF16),
            pltpu.VMEM((TILE, TILE), BF16),
            pltpu.VMEM((1, PART), BF16),
            dma(()),
            dma((3,)),
            dma((CHUNKS,)),
            dma(()),
            dma((5,)),
            dma((CHUNKS, len(GROUPS))),
        ],
        compiler_params=pltpu.CompilerParams(
            collective_id=0, has_side_effects=True, vmem_limit_bytes=56 << 20
        ),
        cost_estimate=pl.CostEstimate(
            flops=2 * 3 * TOK * D * H_DEV, bytes_accessed=3 * 2 * D * H_DEV, transcendentals=TOK * H_DEV
        ),
        name="relayed_feed_forward",
    )(fresh_input, previous_out, norm_gain, gate_weight, up_weight, down_weight)


def solution(mesh):
    in_specs = (
        P(None, "tp"),
        P("section", "tp"),
        P("section", "tp"),
        P("section", None, "tp"),
        P("section", None, "tp"),
        P("section", "tp", None),
    )
    return jax.shard_map(local, mesh=mesh, in_specs=in_specs, out_specs=P("section", "tp"), check_vma=False)
```
